128 devices in a mesh: pipe: 4 (over y), dp: 16 (over x, z), tensor: 2 (over core).
Axes of the slice: x: 4, y: 4, z: 4, core: 2. Of those that a mesh axis runs over, the one named last changes fastest.
Arguments:
- inputs: bfloat16 [4, 512, 4096], P(None, 'dp', 'tensor'), may hold values from -6 to 6
- weights: bfloat16 [4, 4096, 4096], P('pipe', None, 'tensor'), may hold values from -0.09375 to 0.09375
- norm_gains: float32 [4, 4096], P('pipe'), may hold values from 0.5 to 2
- cotangent: bfloat16 [4, 512, 4096], P(None, 'dp', 'tensor'), may hold values from -0.625 to 0.625
- owner_table: int32 [4, 2, 32], P('pipe', 'tensor'), may hold values from 0 to 31, each once within a row
- left_roots: float32 [4, 2, 32, 512, 512], P('pipe', 'tensor', 'dp'), may hold values from -3 to 5, as said below
- right_roots: float32 [4, 2, 32, 512, 512], P('pipe', 'tensor', 'dp'), may hold values from -3 to 5, as said below
Outputs:
- precond_update: bfloat16 [4, 4096, 4096], P('pipe', 'dp', 'tensor')
The draws below stay inside these ranges and needn't reach their ends.
Inputs may be any that keep to these rules, and one draw needn't show every extreme that they name: `owner_table`: for each section and part, every slot number appears once; slot q lives on dp index q // 2. `left_roots`: symmetric matrices. `right_roots`: symmetric matrices.
All inputs are finite; a program needn't handle non-finite values.
Results may differ from the reference program's by a relative error of at most 0.025.
Values may be sent and summed in bfloat16 or wider, within the bound.
A program may use at most 192 MiB of HBM per device.

```python
import math
import jax
import jax.numpy as jnp
from jax import lax

D = 4096
BLK = 512
MB = 4
TOK_DEV = 32
SECTIONS = 4
SPLITS = 2
TOKENS = 512
GROUP_BLOCKS = 32
N_DP = 16


def draw_root(key, diag_low, diag_high, spread):
    diag_key = jax.random.fold_in(key, 1)
    noise_key = jax.random.fold_in(key, 2)
    shape = (SECTIONS, SPLITS, GROUP_BLOCKS, BLK)
    log_diag = jax.random.uniform(diag_key, shape, jnp.float32, jnp.log(diag_low), jnp.log(diag_high))
    noise = jax.random.truncated_normal(noise_key, -4.0, 4.0, shape + (BLK,), jnp.float32)
    noise = noise * (spread / BLK ** 0.5)
    symmetric = (noise + jnp.swapaxes(noise, -1, -2)) * 0.7071
    return symmetric + jnp.exp(log_diag)[..., None] * jnp.eye(BLK, dtype=jnp.float32)


def draw_left_roots(key, part):
    key = jax.random.fold_in(key, 11)
    return draw_root(key, 0.4, 2.5, 0.6)


def draw_right_roots(key, part):
    key = jax.random.fold_in(key, 23)
    return draw_root(key, 0.4, 2.5, 0.6)


def block_levels(rng, dims, pieces, low, high):
    level = 1.0
    for position, blocks in pieces:
        draws = jax.random.uniform(jax.random.fold_in(jax.random.fold_in(rng, 6), position), (blocks,), jnp.float32, low / len(pieces), high / len(pieces))
        level = level * jnp.repeat(jnp.exp(draws), dims[position] // blocks).reshape((-1,) + (1,) * (len(dims) - 1 - position))
    return level


def centred(rng, extent, scale, bound, shards=(), kind=jnp.bfloat16):
    array = jax.random.normal(rng, extent, jnp.float32) * scale
    if len(shards) > 0:
        array = block_levels(rng, extent, shards, -0.22, 0.18) * array
    return jnp.clip(array, min=-bound, max=bound).astype(kind)


def setup_inputs(seed: int = 0) -> dict:
    keys = jax.random.split(jax.random.key(seed), 8)
    inputs = centred(keys[0], (MB, TOKENS, D), 1.0, 6.0, ((1, 16), (2, 2)))
    weights = centred(keys[1], (SECTIONS, D, D), D ** -0.5, 0.09375, ((0, 4), (2, 2)))
    norm_gains = jnp.clip(jnp.exp(math.log(2.0) - 1.3862944 * jax.random.uniform(keys[2], (SECTIONS, D), jnp.float32) ** block_levels(keys[2], (SECTIONS, D), ((0, 4),), -0.2, 0.2)), 0.5, 2.0)
    cotangent = centred(keys[3], (MB, TOKENS, D), 0.04, 0.625, ((1, 16), (2, 2)))
    owner_table = jax.vmap(lambda own: jax.random.permutation(own, GROUP_BLOCKS))(jax.random.split(keys[4], SECTIONS * SPLITS)).reshape((SECTIONS, SPLITS, GROUP_BLOCKS)).astype(jnp.int32)
    left_roots = draw_left_roots(jax.random.fold_in(keys[7], 71), 0)
    right_roots = draw_right_roots(jax.random.fold_in(keys[7], 71), 0)
    return dict(inputs=inputs, weights=weights, norm_gains=norm_gains, cotangent=cotangent, owner_table=owner_table, left_roots=left_roots, right_roots=right_roots)


norm_eps = 1e-05

def section_forward(states, weight, gain):
    states_f = states.astype(jnp.float32)
    inv_rms = lax.rsqrt(lax.optimization_barrier(jnp.mean(states_f * states_f, axis=1, keepdims=True)) + norm_eps)
    normed = (states_f * inv_rms * gain).astype(jnp.bfloat16)
    pre_act = jnp.dot(normed, weight, preferred_element_type=jnp.float32)
    result = (states_f + jax.nn.silu(pre_act)).astype(jnp.bfloat16)
    return (result, normed, pre_act, inv_rms)

def group_sum(normed, dpre):
    width = normed.shape[1]
    norm_groups = normed.reshape(MB, N_DP, TOK_DEV, width).transpose(1, 0, 2, 3).reshape(N_DP, MB * TOK_DEV, width)
    grad_groups = dpre.reshape(MB, N_DP, TOK_DEV, width).transpose(1, 0, 2, 3).reshape(N_DP, MB * TOK_DEV, width)

    def add_group(total, pair):
        partial_sum = lax.dot_general(pair[0], pair[1], (((0,), (0,)), ((), ())), preferred_element_type=jnp.float32)
        rounded = lax.optimization_barrier(partial_sum.astype(jnp.bfloat16))
        return (total + rounded.astype(jnp.float32), None)
    total, unused = lax.scan(add_group, jnp.zeros((width, width), jnp.float32), (norm_groups, grad_groups))
    return lax.optimization_barrier(total.astype(jnp.bfloat16))

def precondition(grad, order, left_set, right_set):
    half_width = D // SPLITS
    row_bands = D // BLK
    col_blocks = half_width // BLK
    outputs = []
    for part_idx in range(SPLITS):
        part_grad = grad[:, part_idx * half_width:(part_idx + 1) * half_width]
        blocks = part_grad.reshape(row_bands, BLK, col_blocks, BLK).transpose(0, 2, 1, 3).reshape(GROUP_BLOCKS, BLK, BLK)
        blocks = blocks.astype(jnp.float32)
        left_pick = left_set[part_idx][order[part_idx]]
        right_pick = right_set[part_idx][order[part_idx]]
        lefted = jnp.einsum('bij,bjk->bik', left_pick, blocks, precision=lax.Precision.HIGHEST)
        result = jnp.einsum('bij,bjk->bik', lefted, right_pick, precision=lax.Precision.HIGHEST).astype(jnp.bfloat16)
        outputs.append(result.reshape(row_bands, col_blocks, BLK, BLK).transpose(0, 2, 1, 3).reshape(D, half_width))
    return jnp.concatenate(outputs, axis=1)

def reference(inputs, weights, norm_gains, cotangent, owner_table, left_roots, right_roots):
    states = inputs.reshape(MB * TOKENS, D)
    saved = []
    for section_idx in range(SECTIONS):
        result, normed, pre_act, inv_rms = section_forward(states, weights[section_idx], norm_gains[section_idx])
        saved.append((states, normed, pre_act, inv_rms))
        states = result
    grad_states = cotangent.reshape(MB * TOKENS, D)
    updates = [None] * SECTIONS
    for section_idx in range(SECTIONS - 1, -1, -1):
        states, normed, pre_act, inv_rms = saved[section_idx]
        grad_f = grad_states.astype(jnp.float32)
        logistic = jax.nn.sigmoid(pre_act)
        dpre = (grad_f * logistic * (1.0 + pre_act * (1.0 - logistic))).astype(jnp.bfloat16)
        dnormed = lax.dot_general(dpre, weights[section_idx], (((1,), (1,)), ((), ())), preferred_element_type=jnp.float32)
        upstream = norm_gains[section_idx] * dnormed
        scaled_states = states.astype(jnp.float32) * inv_rms
        statistic = lax.optimization_barrier(jnp.mean(upstream * scaled_states, axis=1, keepdims=True))
        dstates = inv_rms * (upstream - scaled_states * statistic)
        grad_states = (grad_f + dstates).astype(jnp.bfloat16)
        grad = group_sum(normed, dpre)
        updates[section_idx] = precondition(grad, owner_table[section_idx], left_roots[section_idx], right_roots[section_idx])
    return jnp.stack(updates, axis=0)
```

```python
import functools

import jax
import jax.numpy as jnp
from jax import lax
from jax.experimental import pallas as pl
from jax.experimental.pallas import tpu as pltpu
from jax.sharding import PartitionSpec as P

MESH = pl.DeviceIdType.MESH
norm_eps = 1e-05
GROUPS = ((0, 48), (48, 48), (96, 32))
N_GROUPS = len(GROUPS)
CHUNK = 512
N_CHUNKS = 4
DIRECT = (N_GROUPS - 1,)


def remote(src, dst, send, recv, target):
    return pltpu.make_async_remote_copy(
        src_ref=src, dst_ref=dst, send_sem=send, recv_sem=recv, device_id=target, device_id_type=MESH
    )


def each(low, high, body):
    def step(index, carry):
        body(index)
        return carry

    lax.fori_loop(low, high, step, 0)


def plan_of(section):
    groups = range(N_GROUPS)

    def every(kind):
        return [kind + str(i) for i in groups]

    plan = ["R1"] + ["T"] * (section >= 2)
    if section == 3:
        for i in groups:
            plan += ["F%d" % i, "B%d" % i]
            plan += ["R2"] * (i == 0)
            plan += ["X%d" % i]
        for i in groups:
            plan += ["d%d" % i, "n%d" % i]
        plan += ["N", "U"] + every("G")
    else:
        for i in groups:
            plan += ["F%d" % i, "X%d" % i]
        if section == 0:
            plan += every("n") + ["R2", "N", "U"]
            for i in groups:
                plan += ["B%d" % i]
                if i < N_GROUPS - 1:
                    plan += ["d%d" % i] + ["G%d" % (i - 1)] * (i > 0)
            plan += ["d%d" % (N_GROUPS - 1)]
        elif section == 1:
            plan += ["T"] + every("n") + ["R2"]
            for i in groups:
                plan += ["B%d" % i] + ["d%d" % (i - 1)] * (i > 0)
            plan += ["d%d" % (N_GROUPS - 1), "N", "U"]
        else:
            plan += ["R2"]
            for i in groups:
                plan += ["B%d" % i, "n%d" % i] + ["d%d" % (i - 1)] * (i > 0)
            plan += ["d%d" % (N_GROUPS - 1), "N", "U"]
        plan += [name for name in every("G") if name not in plan]
    plan += ["E"]
    return [name for name in plan if name not in ["d%d" % i for i in DIRECT]]


def kernel(
    order, inputs, weight_hbm, gain, cotangent, left_hbm, right_hbm, out,
    w, wt, h_in, h_sib, h_out, normed, pre, slope, scales, g_in, g_out, dns_out, dns_in, stat_out, stat_in, dpre,
    nrm, dpa, total, stage, frag_out, frag_mid, packed, roots, blocks,
    w_sem, io_sem, stage_sem, yf_s, yf_r, sh_s, sh_r, yb_s, yb_r, dn_s, dn_r, st_s, st_r,
    nr_s, nr_r, ns_s, ns_r, dp_s, dp_r, ds_s, ds_r, sn_s, sn_r, r1_s, r1_r, r2_s, r2_r, fin_s, fin_r,
):
    y = lax.axis_index("pipe")
    k = lax.axis_index("dp")
    t = lax.axis_index("tensor")
    x, z = k // 4, lax.rem(k, 4)
    half = w.shape[1]
    width = w.shape[0]
    block = 512
    frag_rows = 80
    sibling = {"tensor": 1 - t}
    up = {"pipe": lax.rem(y + 1, 4)}
    down = {"pipe": lax.rem(y + 3, 4)}

    def peer(j):
        px = lax.rem(x + j // 4, 4)
        pz = lax.rem(z + lax.rem(j, 4), 4)
        return px, pz, {"dp": px * 4 + pz}

    own0 = pl.multiple_of(t * half, half)
    oth0 = pl.multiple_of((1 - t) * half, half)

    def w_copy(c):
        start = jnp.where(c < N_CHUNKS, own0, oth0) + lax.rem(c, N_CHUNKS) * CHUNK
        rows = pl.ds(pl.multiple_of(start, CHUNK), CHUNK)
        return pltpu.make_async_copy(weight_hbm.at[rows], w.at[rows], w_sem.at[c])

    def stage_copy(i):
        source = (left_hbm, right_hbm)[i % 2]
        return pltpu.make_async_copy(source.at[i // 2], stage.at[i % 2], stage_sem.at[i])

    in_copy = pltpu.make_async_copy(inputs, h_in, io_sem.at[0])
    cot_copy = pltpu.make_async_copy(cotangent, g_in, io_sem.at[1])

    @pl.when(y == 0)
    def _():
        in_copy.start()

    @pl.when(y == 3)
    def _():
        cot_copy.start()

    for i in range(2):
        stage_copy(i).start()
    each(0, 2 * N_CHUNKS, lambda c: w_copy(c).start())

    barrier = pltpu.get_barrier_semaphore()
    for target in (sibling, up, down):
        pl.semaphore_signal(barrier, inc=1, device_id=target, device_id_type=MESH)
    each(1, 16, lambda j: pl.semaphore_signal(barrier, inc=1, device_id=peer(j)[2], device_id_type=MESH))
    pl.semaphore_wait(barrier, 18)

    def cols(c):
        return pl.ds(c * CHUNK, CHUNK)

    def forward_copy(i, c):
        off, m = GROUPS[i]
        n = i * N_CHUNKS + c
        rows = pl.ds(off, m)
        return remote(h_out.at[rows, cols(c)], h_in.at[rows, cols(c)], yf_s.at[n], yf_r.at[n], up)

    def share_copy(i, c):
        off, m = GROUPS[i]
        n = i * N_CHUNKS + c
        rows = pl.ds(off, m)
        return remote(h_in.at[rows, cols(c)], h_sib.at[rows, cols(c)], sh_s.at[n], sh_r.at[n], sibling)

    def backward_copy(i, c):
        off, m = GROUPS[i]
        n = i * N_CHUNKS + c
        rows = pl.ds(off, m)
        return remote(g_out.at[rows, cols(c)], g_in.at[rows, cols(c)], yb_s.at[n], yb_r.at[n], down)

    def dnorm_copy(i, c):
        off, m = GROUPS[i]
        n = i * N_CHUNKS + c
        rows = pl.ds(off, m)
        return remote(dns_out.at[rows, cols(c)], dns_in.at[rows, cols(c)], dn_s.at[n], dn_r.at[n], sibling)

    def stat_copy(i):
        rows = pl.ds(*GROUPS[i])
        return remote(stat_out.at[rows], stat_in.at[rows], st_s.at[i], st_r.at[i], sibling)

    own_band = pl.ds(pl.multiple_of(t * block, block), block)

    def normed_copy(i, d):
        px, pz, target = peer(4 * d)
        columns = pl.ds(pl.multiple_of((2 * px + t) * block, block), block)
        n = i * 4 + d
        return remote(
            normed.at[pl.ds(*GROUPS[i]), columns], nrm[i].at[d, 0, :, own_band], nr_s.at[n], nr_r.at[n], target
        )

    def normed_spread(i, d):
        n = i * 4 + d
        return remote(
            nrm[i].at[:, 0, :, own_band], nrm[i].at[:, d, :, own_band], ns_s.at[n], ns_r.at[n], peer(d)[2]
        )

    def relay_copy(i):
        part = nrm[i].at[:, :, :, own_band]
        return remote(part, part, sn_s.at[i], sn_r.at[i], sibling)

    def dpre_copy(i, j):
        px, pz, target = peer(j)
        columns = pl.ds(pl.multiple_of(pz * block, block), block)
        n = i * 16 + j
        return remote(
            dpre.at[pl.ds(*GROUPS[i]), columns], dpa[i].at[j // 4, lax.rem(j, 4)], dp_s.at[n], dp_r.at[n], target
        )

    def dpre_spread(i, d):
        n = i * 4 + d
        return remote(dpa[i].at[0], dpa[i].at[d], ds_s.at[n], ds_r.at[n], peer(4 * d)[2])

    def dpre_peers(i):
        return 16 if i in DIRECT else 4

    def scatter_copy(j):
        px, pz, target = peer(j)
        return remote(
            frag_out.at[px * 4 + pz], frag_mid.at[pl.ds(2 * k, 2)], r1_s.at[j], r1_r.at[j], target
        )

    def gather_copy(j):
        px, pz, target = peer(j)
        rows = pl.ds(pl.multiple_of(k * frag_rows, frag_rows), frag_rows)
        return remote(frag_out.at[px * 4 + pz], packed.at[:, rows], r2_s.at[j], r2_r.at[j], target)

    def final_copy(d):
        pz = lax.rem(z + d, 4)
        rows = pl.ds(pl.multiple_of(pz * 256, 256), 256)
        columns = pl.ds(pl.multiple_of(z * block, block), block)
        return remote(blocks.at[rows], out.at[:, columns], fin_s.at[d], fin_r.at[d], {"dp": x * 4 + pz})

    def roots_out():
        for i in range(4):
            stage_copy(i).wait()
            values = stage[i % 2].astype(jnp.bfloat16)
            corners = jnp.concatenate([values[128:256, 128:256], values[384:, 384:]], axis=1)
            upper = [values[:128, :256], values[:128, 256:], values[128:256, 256:], values[256:384, 256:], corners]
            first = 8 * (i % 2)
            frag_out[first : first + 8, i // 2] = jnp.concatenate(upper, axis=0).reshape(8, frag_rows, 256)
            if i < 2:
                stage_copy(i + 2).start()
        each(1, 16, lambda j: scatter_copy(j).start())
        frag_mid[pl.ds(2 * k, 2)] = frag_out[k]

    def roots_on():
        each(1, 16, lambda j: scatter_copy(j).wait_send())
        each(1, 16, lambda j: scatter_copy(j).wait_recv())

        def pick(j):
            px, pz, unused = peer(j)
            for i in range(2):
                slot = order[(2 * px + i) * 4 + pz]
                frag_out[px * 4 + pz, i] = frag_mid[slot]

        each(0, 16, pick)
        each(1, 16, lambda j: gather_copy(j).start())
        rows = pl.ds(pl.multiple_of(k * frag_rows, frag_rows), frag_rows)
        packed[:, rows] = frag_out[k]

    def unpack():
        each(1, 16, lambda j: gather_copy(j).wait_recv())

        def one(n):
            i, side = n // 2, lax.rem(n, 2)
            root = roots.at[i, side]
            squares = {}
            for r, (first, second) in enumerate((((0, 0), (0, 1)), ((0, 2), (0, 3)), ((1, 2), (1, 3)), ((2, 2), (2, 3)), ((1, 1), (3, 3)))):
                rows = packed[i, pl.ds(pl.multiple_of(side * 640 + r * 128, 128), 128), :]
                squares[first] = rows[:, :128]
                squares[second] = rows[:, 128:]
            for (a, b), square in squares.items():
                root[a * 128 : a * 128 + 128, b * 128 : b * 128 + 128] = square
                if a != b:
                    root[b * 128 : b * 128 + 128, a * 128 : a * 128 + 128] = square.T

        each(0, 4, one)

    def transpose_weight():
        @pl.when(y >= 2)
        def _():
            each(0, 2 * N_CHUNKS, lambda c: w_copy(c).wait())

        def turn(c):
            part = pl.ds(pl.multiple_of(c * 256, 256), 256)
            wt[:, part] = w[part, :].T

        each(0, width // 256, turn)

    def forward(i):
        off, m = GROUPS[i]
        rows = pl.ds(off, m)
        if i == 0:
            @pl.when(y == 0)
            def _():
                in_copy.wait()
        squares = jnp.zeros((m, 1), jnp.float32)
        for c in range(N_CHUNKS):
            @pl.when(y > 0)
            def _():
                forward_copy(i, c).wait_recv()

            share_copy(i, c).start()
            if i == 0:
                @pl.when(y < 2)
                def _():
                    w_copy(c).wait()
            states = h_in[rows, cols(c)].astype(jnp.float32)
            squares += jnp.sum(states * states, axis=1, keepdims=True)
            place = pl.multiple_of(own0 + c * CHUNK, CHUNK)
            gained = (states * gain[:, pl.ds(place, CHUNK)]).astype(jnp.bfloat16)
            product = jnp.dot(gained, w[pl.ds(place, CHUNK), :], preferred_element_type=jnp.float32)
            pre[rows, :] = product if c == 0 else pre[rows, :] + product
        for c in range(N_CHUNKS):
            share_copy(i, c).wait_recv()
            if i == 0:
                @pl.when(y < 2)
                def _():
                    w_copy(N_CHUNKS + c).wait()
            states = h_sib[rows, cols(c)].astype(jnp.float32)
            squares += jnp.sum(states * states, axis=1, keepdims=True)
            place = pl.multiple_of(oth0 + c * CHUNK, CHUNK)
            gained = (states * gain[:, pl.ds(place, CHUNK)]).astype(jnp.bfloat16)
            if c < N_CHUNKS - 1:
                product = jnp.dot(gained, w[pl.ds(place, CHUNK), :], preferred_element_type=jnp.float32)
                pre[rows, :] += product
        scale = lax.rsqrt(squares / width + norm_eps)
        scales[rows, :] = jnp.broadcast_to(scale, (m, 128))
        for c in range(N_CHUNKS):
            product = jnp.dot(gained, w[pl.ds(place, CHUNK), cols(c)], preferred_element_type=jnp.float32)
            value = scale * (pre[rows, cols(c)] + product)
            logistic = 1.0 / (1.0 + jnp.exp(-value))
            h_out[rows, cols(c)] = (h_in[rows, cols(c)].astype(jnp.float32) + value * logistic).astype(jnp.bfloat16)

            @pl.when(y < 3)
            def _():
                forward_copy(i, c).start()

            pre[rows, cols(c)] = value
            slope[rows, cols(c)] = logistic * (1.0 + value * (1.0 - logistic))

    def normalise(i):
        off, m = GROUPS[i]
        rows = pl.ds(off, m)
        scale = scales[rows, 0:1]
        for c in range(N_CHUNKS):
            for source, first in ((h_in, own0), (h_sib, oth0)):
                columns = pl.ds(pl.multiple_of(first + c * CHUNK, CHUNK), CHUNK)
                states = source[rows, cols(c)].astype(jnp.float32)
                normed[rows, columns] = (states * scale * gain[:, columns]).astype(jnp.bfloat16)
        each(1, 4, lambda d: normed_copy(i, d).start())
        nrm[i][0, 0, :, own_band] = normed[rows, pl.ds(pl.multiple_of((2 * x + t) * block, block), block)]

    def normed_on(i):
        each(1, 4, lambda d: normed_copy(i, d).wait_recv())
        each(1, 4, lambda d: normed_spread(i, d).start())

    def backward(i):
        off, m = GROUPS[i]
        rows = pl.ds(off, m)
        if i == 0:
            @pl.when(y == 3)
            def _():
                cot_copy.wait()
        stat = jnp.zeros((m, 1), jnp.float32)
        for c in range(N_CHUNKS):
            @pl.when(y < 3)
            def _():
                backward_copy(i, c).wait_recv()

            grads = (g_in[rows, cols(c)].astype(jnp.float32) * slope[rows, cols(c)]).astype(jnp.bfloat16)
            dpre[rows, cols(c)] = grads
            stat += jnp.sum(grads.astype(jnp.float32) * pre[rows, cols(c)], axis=1, keepdims=True)

        @pl.when(y > 0)
        def _():
            stat_out[rows, :] = jnp.broadcast_to(stat, (m, 128))
            stat_copy(i).start()

        each(1, dpre_peers(i), lambda j: dpre_copy(i, j).start())
        dpa[i][0, 0] = dpre[rows, pl.ds(pl.multiple_of(z * block, block), block)]

        @pl.when(y > 0)
        def _():
            for c in range(N_CHUNKS):
                columns = pl.ds(pl.multiple_of(oth0 + c * CHUNK, CHUNK), CHUNK)
                part = jnp.dot(dpre[rows, :], wt[:, columns], preferred_element_type=jnp.float32)
                dns_out[rows, cols(c)] = part.astype(jnp.bfloat16)
                dnorm_copy(i, c).start()
            stat_copy(i).wait_recv()
            scale = scales[rows, 0:1]
            mean = (stat_out[rows, 0:1] + stat_in[rows, 0:1]) / width
            for c in range(N_CHUNKS):
                columns = pl.ds(pl.multiple_of(own0 + c * CHUNK, CHUNK), CHUNK)
                part = jnp.dot(dpre[rows, :], wt[:, columns], preferred_element_type=jnp.float32)
                dnorm_copy(i, c).wait_recv()
                part += dns_in[rows, cols(c)].astype(jnp.float32)
                states = h_in[rows, cols(c)].astype(jnp.float32)
                dstates = scale * (part * gain[:, columns] - states * scale * mean)
                g_out[rows, cols(c)] = (g_in[rows, cols(c)].astype(jnp.float32) + dstates).astype(jnp.bfloat16)
                backward_copy(i, c).start()

    def dpre_on(i):
        each(1, dpre_peers(i), lambda j: dpre_copy(i, j).wait_recv())
        each(1, 4, lambda d: dpre_spread(i, d).start())

    def relay():
        for i in range(N_GROUPS):
            each(1, 4, lambda d: normed_spread(i, d).wait_recv())
            relay_copy(i).start()

    def gradient(i):
        m = GROUPS[i][1]
        relay_copy(i).wait_recv()
        if i in DIRECT:
            each(1, 16, lambda j: dpre_copy(i, j).wait_recv())
        else:
            each(1, 4, lambda d: dpre_spread(i, d).wait_recv())
        right = dpa[i][...].reshape(16 * m, block)
        for c in range(4):
            part = pl.ds(c * 256, 256)
            left = nrm[i][:, :, :, part].reshape(16 * m, 256)
            product = lax.dot_general(left, right, (((0,), (0,)), ((), ())), preferred_element_type=jnp.float32)
            total[part, :] = product if i == 0 else total[part, :] + product

    def precondition():
        for i in range(2):
            grad = total[pl.ds(i * block, block), :].astype(jnp.bfloat16)
            lefted = jnp.dot(roots[i, 0], grad, preferred_element_type=jnp.float32).astype(jnp.bfloat16)
            result = jnp.dot(lefted, roots[i, 1], preferred_element_type=jnp.float32).astype(jnp.bfloat16)
            blocks[pl.ds(i * block, block), :] = result
            for d in range(1, 4):
                @pl.when(lax.rem(z + d, 4) // 2 == i)
                def _():
                    final_copy(d).start()
        columns = pl.ds(pl.multiple_of(z * block, block), block)
        out[:, columns] = blocks[pl.ds(pl.multiple_of(z * 256, 256), 256), :]

        for i in range(N_GROUPS):
            for c in range(N_CHUNKS):
                share_copy(i, c).wait_send()

                @pl.when(y < 3)
                def _():
                    forward_copy(i, c).wait_send()

                @pl.when(y > 0)
                def _():
                    backward_copy(i, c).wait_send()
                    dnorm_copy(i, c).wait_send()

            @pl.when(y > 0)
            def _():
                stat_copy(i).wait_send()

            relay_copy(i).wait_send()
            each(1, 4, lambda d: normed_copy(i, d).wait_send())
            each(1, 4, lambda d: normed_spread(i, d).wait_send())
            each(1, dpre_peers(i), lambda j: dpre_copy(i, j).wait_send())
            if i not in DIRECT:
                each(1, 4, lambda d: dpre_spread(i, d).wait_send())
        each(1, 16, lambda j: gather_copy(j).wait_send())
        for d in range(1, 4):
            final_copy(d).wait_send()
        for d in range(1, 4):
            final_copy(d).wait_recv()

    ops = dict(R1=roots_out, R2=roots_on, U=unpack, T=transpose_weight, N=relay, E=precondition)
    kinds = dict(F=forward, X=normalise, n=normed_on, B=backward, d=dpre_on, G=gradient)
    for i in range(N_GROUPS):
        for kind, op in kinds.items():
            if kind != "d" or i not in DIRECT:
                ops[kind + str(i)] = functools.partial(op, i)
    plans = [plan_of(section) for section in range(4)]

    def step(s):
        for name, op in ops.items():
            place = [plan.index(name) if name in plan else -1 for plan in plans]
            mine = jnp.int32(place[3])
            for section in (2, 1, 0):
                mine = jnp.where(y == section, place[section], mine)
            pl.when(s == mine)(op)

    each(0, max(len(plan) for plan in plans), step)


def on_device(inputs, weights, norm_gains, cotangent, owner_table, left_roots, right_roots):
    tokens = inputs.shape[0] * inputs.shape[1]
    half = weights.shape[2]
    width = weights.shape[1]
    bf16, f32 = jnp.bfloat16, jnp.float32
    vmem, dma = pltpu.VMEM, pltpu.SemaphoreType.DMA
    steps = N_GROUPS * N_CHUNKS
    scratch = [
        vmem((width, half), bf16), vmem((half, width), bf16),
        vmem((tokens, half), bf16), vmem((tokens, half), bf16), vmem((tokens, half), bf16),
        vmem((tokens, width), bf16), vmem((tokens, half), f32), vmem((tokens, half), f32), vmem((tokens, 128), f32),
        vmem((tokens, half), bf16), vmem((tokens, half), bf16), vmem((tokens, half), bf16), vmem((tokens, half), bf16),
        vmem((tokens, 128), f32), vmem((tokens, 128), f32), vmem((tokens, half), bf16),
        [vmem((4, 4, m, 1024), bf16) for unused, m in GROUPS], [vmem((4, 4, m, 512), bf16) for unused, m in GROUPS],
        vmem((1024, 512), f32), vmem((2, 512, 512), f32),
        vmem((16, 2, 80, 256), bf16), vmem((32, 80, 256), bf16), vmem((2, 1280, 256), bf16),
        vmem((2, 2, 512, 512), bf16),
        vmem((1024, 512), bf16),
        dma((8,)), dma((2,)), dma((4,)),
        dma((steps,)), dma((steps,)), dma((steps,)), dma((steps,)),
        dma((steps,)), dma((steps,)), dma((steps,)), dma((steps,)), dma((N_GROUPS,)), dma((N_GROUPS,)),
        dma((N_GROUPS * 4,)), dma((N_GROUPS * 4,)), dma((N_GROUPS * 4,)), dma((N_GROUPS * 4,)),
        dma((N_GROUPS * 16,)), dma((N_GROUPS * 16,)), dma((N_GROUPS * 4,)), dma((N_GROUPS * 4,)),
        dma((N_GROUPS,)), dma((N_GROUPS,)),
        dma((16,)), dma((16,)), dma((16,)), dma((16,)), dma((4,)), dma((4,)),
    ]
    in_vmem = pl.BlockSpec(memory_space=pltpu.VMEM)
    in_hbm = pl.BlockSpec(memory_space=pl.ANY)
    result = pl.pallas_call(
        kernel,
        out_shape=jax.ShapeDtypeStruct((256, half), bf16),
        in_specs=[pl.BlockSpec(memory_space=pltpu.SMEM), in_hbm, in_hbm, in_vmem, in_hbm, in_hbm, in_hbm],
        out_specs=in_vmem,
        scratch_shapes=scratch,
        compiler_params=pltpu.CompilerParams(
            collective_id=0, has_side_effects=True, vmem_limit_bytes=62 * 2**20
        ),
    )(
        owner_table.reshape(-1), inputs.reshape(tokens, half), weights[0], norm_gains,
        cotangent.reshape(tokens, half), left_roots[0, 0], right_roots[0, 0],
    )
    return result[None]


def solution(mesh):
    return jax.shard_map(
        on_device,
        mesh=mesh,
        in_specs=(
            P(None, "dp", "tensor"),
            P("pipe", None, "tensor"),
            P("pipe", None),
            P(None, "dp", "tensor"),
            P("pipe", "tensor", None),
            P("pipe", "tensor", "dp", None, None),
            P("pipe", "tensor", "dp", None, None),
        ),
        out_specs=P("pipe", "dp", "tensor"),
        check_vma=False,
    )
```

```python
import functools

import jax
import jax.numpy as jnp
from jax import lax
from jax.experimental import pallas as pl
from jax.experimental.pallas import tpu as pltpu
from jax.sharding import PartitionSpec as P

MESH = pl.DeviceIdType.MESH
norm_eps = 1e-05
GROUPS = ((0, 48), (48, 48), (96, 32))
N_GROUPS = len(GROUPS)
CHUNK = 512
N_CHUNKS = 4
DIRECT = (1, 2)


def remote(src, dst, send, recv, target):
    return pltpu.make_async_remote_copy(
        src_ref=src, dst_ref=dst, send_sem=send, recv_sem=recv, device_id=target, device_id_type=MESH
    )


def each(low, high, body):
    def step(index, carry):
        body(index)
        return carry

    lax.fori_loop(low, high, step, 0)


def plan_of(section):
    groups = range(N_GROUPS)

    def every(kind):
        return [kind + str(i) for i in groups]

    if section == 0:
        plan = ["F0", "X0", "R1"]
        for i in groups[1:]:
            plan += ["F%d" % i, "X%d" % i, "n%d" % (i - 1)]
        plan += ["n%d" % (N_GROUPS - 1), "R2"] + every("N")
        for i in groups:
            plan += ["B%d" % i]
            if i < N_GROUPS - 1:
                plan += ["d%d" % i] + ["G%d" % (i - 1)] * (i > 0)
            if i == N_GROUPS - 2:
                plan += ["U"]
        plan += ["d%d" % (N_GROUPS - 1)]
    elif section == 1:
        plan = ["R1"]
        for i in groups:
            plan += ["F%d" % i, "X%d" % i] + (["n%d" % (i - 1)] if i > 0 else ["R2"])
        plan += ["n%d" % (N_GROUPS - 1), "T"]
        for i in groups:
            plan += ["B%d" % i, "d%d" % i]
        plan += every("N") + ["U"]
    elif section == 2:
        plan = ["R1", "T"]
        for i in groups:
            plan += ["F%d" % i, "X%d" % i] + ["R2"] * (i == 0)
        for i in groups:
            plan += ["B%d" % i, "n%d" % i] + ["d%d" % (i - 1)] * (i > 0)
        plan += ["d%d" % (N_GROUPS - 1)] + every("N") + ["U"]
    else:
        plan = ["R1", "T", "R2"]
        for i in groups:
            plan += ["F%d" % i, "B%d" % i, "X%d" % i]
            if i > 0:
                plan += ["n%d" % (i - 1), "d%d" % (i - 1)]
        plan += ["n%d" % (N_GROUPS - 1), "d%d" % (N_GROUPS - 1)] + every("N") + ["U"]
    plan += [name for name in every("G") if name not in plan]
    plan += ["E"]
    return [name for name in plan if name not in ["d%d" % i for i in DIRECT]]


def kernel(
    order, inputs, weight_hbm, gain, cotangent, left_hbm, right_hbm, out_left, out_right,
    w, wt, h_in, h_sib, h_out, normed, pre, slope, scales, g_in, g_out, dns_out, dns_in, stat_out, stat_in, dpre,
    nrm, dpa, total, stage, frag_out, frag_mid, diag_mid, packed, roots, blocks,
    w_sem, io_sem, stage_sem, yf_s, yf_r, sh_s, sh_r, yb_s, yb_r, dn_s, dn_r, st_s, st_r,
    nr_s, nr_r, ns_s, ns_r, dp_s, dp_r, ds_s, ds_r, sn_s, sn_r, r1_s, r1_r, rd_s, rd_r, r2_s, r2_r, fin_s, fin_r,
):
    y = lax.axis_index("pipe")
    k = lax.axis_index("dp")
    t = lax.axis_index("tensor")
    x, z = k // 4, lax.rem(k, 4)
    half = w.shape[1]
    width = w.shape[0]
    block = 512
    frag_rows = 64
    sibling = {"tensor": 1 - t}
    up = {"pipe": lax.rem(y + 1, 4)}
    down = {"pipe": lax.rem(y + 3, 4)}

    def peer(j):
        px = lax.rem(x + j // 4, 4)
        pz = lax.rem(z + lax.rem(j, 4), 4)
        return px, pz, {"dp": px * 4 + pz}

    own0 = pl.multiple_of(t * half, half)
    oth0 = pl.multiple_of((1 - t) * half, half)

    def w_copy(c):
        start = jnp.where(c < N_CHUNKS, own0, oth0) + lax.rem(c, N_CHUNKS) * CHUNK
        rows = pl.ds(pl.multiple_of(start, CHUNK), CHUNK)
        return pltpu.make_async_copy(weight_hbm.at[rows], w.at[rows], w_sem.at[c])

    def stage_copy(i):
        source = (left_hbm, right_hbm)[i % 2]
        return pltpu.make_async_copy(source.at[i // 2], stage.at[i % 2], stage_sem.at[i])

    in_copy = pltpu.make_async_copy(inputs, h_in, io_sem.at[0])
    cot_copy = pltpu.make_async_copy(cotangent, g_in, io_sem.at[1])

    @pl.when(y == 0)
    def _():
        in_copy.start()

    @pl.when(y == 3)
    def _():
        cot_copy.start()

    def stage_start():
        for i in range(2):
            stage_copy(i).start()

    pl.when(y > 0)(stage_start)
    each(0, 2 * N_CHUNKS, lambda c: w_copy(c).start())
    pl.when(y == 0)(stage_start)

    barrier = pltpu.get_barrier_semaphore()
    for target in (sibling, up, down):
        pl.semaphore_signal(barrier, inc=1, device_id=target, device_id_type=MESH)
    each(1, 16, lambda j: pl.semaphore_signal(barrier, inc=1, device_id=peer(j)[2], device_id_type=MESH))
    pl.semaphore_wait(barrier, 18)

    def cols(c):
        return pl.ds(c * CHUNK, CHUNK)

    def forward_copy(i, c):
        off, m = GROUPS[i]
        n = i * N_CHUNKS + c
        rows = pl.ds(off, m)
        return remote(h_out.at[rows, cols(c)], h_in.at[rows, cols(c)], yf_s.at[n], yf_r.at[n], up)

    def share_copy(i, c):
        off, m = GROUPS[i]
        n = i * N_CHUNKS + c
        rows = pl.ds(off, m)
        return remote(h_in.at[rows, cols(c)], h_sib.at[rows, cols(c)], sh_s.at[n], sh_r.at[n], sibling)

    def backward_copy(i, c):
        off, m = GROUPS[i]
        n = i * N_CHUNKS + c
        rows = pl.ds(off, m)
        return remote(g_out.at[rows, cols(c)], g_in.at[rows, cols(c)], yb_s.at[n], yb_r.at[n], down)

    def dnorm_copy(i, c):
        off, m = GROUPS[i]
        n = i * N_CHUNKS + c
        rows = pl.ds(off, m)
        return remote(dns_out.at[rows, cols(c)], dns_in.at[rows, cols(c)], dn_s.at[n], dn_r.at[n], sibling)

    def stat_copy(i):
        rows = pl.ds(*GROUPS[i])
        return remote(stat_out.at[rows], stat_in.at[rows], st_s.at[i], st_r.at[i], sibling)

    own_band = pl.ds(pl.multiple_of(t * block, block), block)

    def normed_copy(i, d):
        px, pz, target = peer(4 * d)
        columns = pl.ds(pl.multiple_of((2 * px + t) * block, block), block)
        n = i * 4 + d
        return remote(
            normed.at[pl.ds(*GROUPS[i]), columns], nrm[i].at[d, 0, :, own_band], nr_s.at[n], nr_r.at[n], target
        )

    def normed_spread(i, d):
        n = i * 4 + d
        return remote(
            nrm[i].at[:, 0, :, own_band], nrm[i].at[:, d, :, own_band], ns_s.at[n], ns_r.at[n], peer(d)[2]
        )

    def relay_copy(i):
        part = nrm[i].at[:, :, :, own_band]
        return remote(part, part, sn_s.at[i], sn_r.at[i], sibling)

    def dpre_copy(i, j):
        px, pz, target = peer(j)
        columns = pl.ds(pl.multiple_of(pz * block, block), block)
        n = i * 16 + j
        return remote(
            dpre.at[pl.ds(*GROUPS[i]), columns], dpa[i].at[j // 4, lax.rem(j, 4)], dp_s.at[n], dp_r.at[n], target
        )

    def dpre_spread(i, d):
        n = i * 4 + d
        return remote(dpa[i].at[0], dpa[i].at[d], ds_s.at[n], ds_r.at[n], peer(4 * d)[2])

    def dpre_peers(i):
        return 16 if i in DIRECT else 4

    def scatter_copy(j):
        px, pz, target = peer(j)
        return remote(
            frag_out.at[px * 4 + pz], frag_mid.at[pl.ds(2 * k, 2)], r1_s.at[j], r1_r.at[j], target
        )

    def diag_copy(j):
        part = diag_mid.at[pl.ds(2 * k, 2)]
        return remote(part, part, rd_s.at[j], rd_r.at[j], peer(j)[2])

    def gather_copy(j):
        px, pz, target = peer(j)
        rows = pl.ds(pl.multiple_of(k * frag_rows, frag_rows), frag_rows)
        return remote(frag_out.at[px * 4 + pz], packed.at[:, rows], r2_s.at[j], r2_r.at[j], target)

    def final_copy(d, out=out_left):
        pz = lax.rem(z + d, 4)
        rows = pl.ds(pl.multiple_of(pz * 256, 256), 256)
        columns = pl.ds(pl.multiple_of(lax.rem(z, 2) * block, block), block)
        return remote(blocks.at[rows], out.at[:, columns], fin_s.at[d], fin_r.at[d], {"dp": x * 4 + pz})

    row_of = lax.broadcasted_iota(jnp.int32, (128, 128), 0)
    col_of = lax.broadcasted_iota(jnp.int32, (128, 128), 1)

    def roots_out():
        for i in range(4):
            stage_copy(i).wait()
            values = stage[i % 2].astype(jnp.bfloat16)

            def square(a, b):
                return values[a * 128 : a * 128 + 128, b * 128 : b * 128 + 128]

            def fold(a, b):
                return jnp.where(col_of >= row_of, square(a, a).astype(jnp.float32), square(b, b).astype(jnp.float32))

            for n in range(2):
                corner = jnp.where(col_of == row_of, square(2 * n + 1, 2 * n + 1).astype(jnp.float32), 0.0)
                row = 2 * (i % 2) + n
                diag_mid[2 * k + i // 2, row : row + 1, :] = jnp.sum(corner, axis=0, keepdims=True)
            upper = [
                values[:128, 128:384],
                jnp.concatenate([square(0, 3), square(1, 2)], axis=1),
                jnp.concatenate([square(1, 3), square(2, 3)], axis=1),
                jnp.concatenate([fold(0, 1), fold(2, 3)], axis=1).astype(jnp.bfloat16),
            ]
            first = 8 * (i % 2)
            frag_out[first : first + 8, i // 2] = jnp.concatenate(upper, axis=0).reshape(8, frag_rows, 256)
            if i < 2:
                stage_copy(i + 2).start()
        each(1, 16, lambda j: scatter_copy(j).start())
        each(1, 16, lambda j: diag_copy(j).start())
        frag_mid[pl.ds(2 * k, 2)] = frag_out[k]

    def roots_on():
        each(1, 16, lambda j: scatter_copy(j).wait_send())
        each(1, 16, lambda j: scatter_copy(j).wait_recv())
        each(1, 16, lambda j: diag_copy(j).wait_send())
        each(1, 16, lambda j: diag_copy(j).wait_recv())

        def pick(j):
            px, pz, unused = peer(j)
            for i in range(2):
                slot = order[(2 * px + i) * 4 + pz]
                frag_out[px * 4 + pz, i] = frag_mid[slot]

        each(0, 16, pick)
        each(1, 16, lambda j: gather_copy(j).start())
        rows = pl.ds(pl.multiple_of(k * frag_rows, frag_rows), frag_rows)
        packed[:, rows] = frag_out[k]

    def unpack():
        each(1, 16, lambda j: gather_copy(j).wait_recv())

        def one(n):
            i, side = n // 2, lax.rem(n, 2)
            root = roots.at[i, side]
            diagonals = diag_mid[order[(2 * x + i) * 4 + z]]

            def place(a, b, square):
                root[a * 128 : a * 128 + 128, b * 128 : b * 128 + 128] = square

            def rows(r):
                return packed[i, pl.ds(pl.multiple_of(side * 512 + r * 128, 128), 128), :]

            for r, pair in enumerate((((0, 1), (0, 2)), ((0, 3), (1, 2)), ((1, 3), (2, 3)))):
                both = rows(r)
                for (a, b), square in zip(pair, (both[:, :128], both[:, 128:])):
                    place(a, b, square)
                    place(b, a, square.T)
            both = rows(3).astype(jnp.float32)
            for m, square in enumerate((both[:, :128], both[:, 128:])):
                turned = square.T
                place(2 * m, 2 * m, jnp.where(col_of >= row_of, square, turned).astype(jnp.bfloat16))
                diagonal = jnp.where(side == 0, diagonals[m : m + 1, :], diagonals[m + 2 : m + 3, :])
                second = jnp.where(col_of < row_of, square, jnp.where(col_of > row_of, turned, diagonal))
                place(2 * m + 1, 2 * m + 1, second.astype(jnp.bfloat16))

        each(0, 4, one)

    def transpose_weight():
        @pl.when(y >= 2)
        def _():
            each(0, 2 * N_CHUNKS, lambda c: w_copy(c).wait())

        def turn(c):
            part = pl.ds(pl.multiple_of(c * 256, 256), 256)
            wt[:, part] = w[part, :].T

        each(0, width // 256, turn)

    def forward(i):
        off, m = GROUPS[i]
        rows = pl.ds(off, m)
        if i == 0:
            @pl.when(y == 0)
            def _():
                in_copy.wait()
        squares = jnp.zeros((m, 1), jnp.float32)
        for c in range(N_CHUNKS):
            @pl.when(y > 0)
            def _():
                forward_copy(i, c).wait_recv()

            share_copy(i, c).start()
            if i == 0:
                @pl.when(y < 2)
                def _():
                    w_copy(c).wait()
            states = h_in[rows, cols(c)].astype(jnp.float32)
            squares += jnp.sum(states * states, axis=1, keepdims=True)
            place = pl.multiple_of(own0 + c * CHUNK, CHUNK)
            gained = (states * gain[:, pl.ds(place, CHUNK)]).astype(jnp.bfloat16)
            product = jnp.dot(gained, w[pl.ds(place, CHUNK), :], preferred_element_type=jnp.float32)
            pre[rows, :] = product if c == 0 else pre[rows, :] + product
        for c in range(N_CHUNKS):
            share_copy(i, c).wait_recv()
            if i == 0:
                @pl.when(y < 2)
                def _():
                    w_copy(N_CHUNKS + c).wait()
            states = h_sib[rows, cols(c)].astype(jnp.float32)
            squares += jnp.sum(states * states, axis=1, keepdims=True)
            place = pl.multiple_of(oth0 + c * CHUNK, CHUNK)
            gained = (states * gain[:, pl.ds(place, CHUNK)]).astype(jnp.bfloat16)
            if c < N_CHUNKS - 1:
                product = jnp.dot(gained, w[pl.ds(place, CHUNK), :], preferred_element_type=jnp.float32)
                pre[rows, :] += product
        scale = lax.rsqrt(squares / width + norm_eps)
        scales[rows, :] = jnp.broadcast_to(scale, (m, 128))
        for c in range(N_CHUNKS):
            product = jnp.dot(gained, w[pl.ds(place, CHUNK), cols(c)], preferred_element_type=jnp.float32)
            value = scale * (pre[rows, cols(c)] + product)
            logistic = 1.0 / (1.0 + jnp.exp(-value))
            h_out[rows, cols(c)] = (h_in[rows, cols(c)].astype(jnp.float32) + value * logistic).astype(jnp.bfloat16)

            @pl.when(y < 3)
            def _():
                forward_copy(i, c).start()

            pre[rows, cols(c)] = value
            slope[rows, cols(c)] = logistic * (1.0 + value * (1.0 - logistic))

    def normalise(i):
        off, m = GROUPS[i]
        rows = pl.ds(off, m)
        scale = scales[rows, 0:1]
        for c in range(N_CHUNKS):
            for source, first in ((h_in, own0), (h_sib, oth0)):
                columns = pl.ds(pl.multiple_of(first + c * CHUNK, CHUNK), CHUNK)
                states = source[rows, cols(c)].astype(jnp.float32)
                normed[rows, columns] = (states * scale * gain[:, columns]).astype(jnp.bfloat16)
        each(1, 4, lambda d: normed_copy(i, d).start())
        nrm[i][0, 0, :, own_band] = normed[rows, pl.ds(pl.multiple_of((2 * x + t) * block, block), block)]

    def normed_on(i):
        each(1, 4, lambda d: normed_copy(i, d).wait_recv())
        each(1, 4, lambda d: normed_spread(i, d).start())

    def backward(i):
        off, m = GROUPS[i]
        rows = pl.ds(off, m)
        if i == 0:
            @pl.when(y == 3)
            def _():
                cot_copy.wait()
        stat = jnp.zeros((m, 1), jnp.float32)
        for c in range(N_CHUNKS):
            @pl.when(y < 3)
            def _():
                backward_copy(i, c).wait_recv()

            grads = (g_in[rows, cols(c)].astype(jnp.float32) * slope[rows, cols(c)]).astype(jnp.bfloat16)
            dpre[rows, cols(c)] = grads
            stat += jnp.sum(grads.astype(jnp.float32) * pre[rows, cols(c)], axis=1, keepdims=True)
            if i in DIRECT:
                ahead = lax.rem(c - z + 4, 4)
                each(1, 4, lambda d: dpre_copy(i, 4 * d + ahead).start())
                pl.when(ahead > 0)(lambda: dpre_copy(i, ahead).start())

        @pl.when(y > 0)
        def _():
            stat_out[rows, :] = jnp.broadcast_to(stat, (m, 128))
            stat_copy(i).start()

        if i not in DIRECT:
            each(1, 4, lambda j: dpre_copy(i, j).start())
        dpa[i][0, 0] = dpre[rows, pl.ds(pl.multiple_of(z * block, block), block)]

        @pl.when(y > 0)
        def _():
            for c in range(N_CHUNKS):
                columns = pl.ds(pl.multiple_of(oth0 + c * CHUNK, CHUNK), CHUNK)
                part = jnp.dot(dpre[rows, :], wt[:, columns], preferred_element_type=jnp.float32)
                dns_out[rows, cols(c)] = part.astype(jnp.bfloat16)
                dnorm_copy(i, c).start()
            stat_copy(i).wait_recv()
            scale = scales[rows, 0:1]
            mean = (stat_out[rows, 0:1] + stat_in[rows, 0:1]) / width
            for c in range(N_CHUNKS):
                columns = pl.ds(pl.multiple_of(own0 + c * CHUNK, CHUNK), CHUNK)
                part = jnp.dot(dpre[rows, :], wt[:, columns], preferred_element_type=jnp.float32)
                dnorm_copy(i, c).wait_recv()
                part += dns_in[rows, cols(c)].astype(jnp.float32)
                states = h_in[rows, cols(c)].astype(jnp.float32)
                dstates = scale * (part * gain[:, columns] - states * scale * mean)
                g_out[rows, cols(c)] = (g_in[rows, cols(c)].astype(jnp.float32) + dstates).astype(jnp.bfloat16)
                backward_copy(i, c).start()

    def dpre_on(i):
        each(1, dpre_peers(i), lambda j: dpre_copy(i, j).wait_recv())
        each(1, 4, lambda d: dpre_spread(i, d).start())

    def relay(i):
        each(1, 4, lambda d: normed_spread(i, d).wait_recv())
        relay_copy(i).start()

    def gradient(i):
        m = GROUPS[i][1]
        relay_copy(i).wait_recv()
        if i in DIRECT:
            each(1, 16, lambda j: dpre_copy(i, j).wait_recv())
        else:
            each(1, 4, lambda d: dpre_spread(i, d).wait_recv())
        right = dpa[i][...].reshape(16 * m, block)
        for c in range(4):
            part = pl.ds(c * 256, 256)
            left = nrm[i][:, :, :, part].reshape(16 * m, 256)
            product = lax.dot_general(left, right, (((0,), (0,)), ((), ())), preferred_element_type=jnp.float32)
            total[part, :] = product if i == 0 else total[part, :] + product

    def precondition():
        for i in range(2):
            grad = total[pl.ds(i * block, block), :].astype(jnp.bfloat16)
            lefted = jnp.dot(roots[i, 0], grad, preferred_element_type=jnp.float32).astype(jnp.bfloat16)
            result = jnp.dot(lefted, roots[i, 1], preferred_element_type=jnp.float32).astype(jnp.bfloat16)
            blocks[pl.ds(i * block, block), :] = result
            for d in range(1, 4):
                for side, out in enumerate((out_left, out_right)):
                    @pl.when((lax.rem(z + d, 4) // 2 == i) & (z // 2 == side))
                    def _():
                        final_copy(d, out).start()

        def keep_copy(out):
            rows = pl.ds(pl.multiple_of(z * 256, 256), 256)
            columns = pl.ds(pl.multiple_of(lax.rem(z, 2) * block, block), block)
            return pltpu.make_async_copy(blocks.at[rows], out.at[:, columns], io_sem.at[0])

        for side, out in enumerate((out_left, out_right)):
            pl.when(z // 2 == side)(lambda: keep_copy(out).start())

        for i in range(N_GROUPS):
            for c in range(N_CHUNKS):
                share_copy(i, c).wait_send()

                @pl.when(y < 3)
                def _():
                    forward_copy(i, c).wait_send()

                @pl.when(y > 0)
                def _():
                    backward_copy(i, c).wait_send()
                    dnorm_copy(i, c).wait_send()

            @pl.when(y > 0)
            def _():
                stat_copy(i).wait_send()

            relay_copy(i).wait_send()
            each(1, 4, lambda d: normed_copy(i, d).wait_send())
            each(1, 4, lambda d: normed_spread(i, d).wait_send())
            each(1, dpre_peers(i), lambda j: dpre_copy(i, j).wait_send())
            if i not in DIRECT:
                each(1, 4, lambda d: dpre_spread(i, d).wait_send())
        each(1, 16, lambda j: gather_copy(j).wait_send())
        for d in range(1, 4):
            final_copy(d).wait_send()
        keep_copy(out_left).wait()
        for d in range(1, 4):
            final_copy(d).wait_recv()

    ops = dict(R1=roots_out, R2=roots_on, U=unpack, T=transpose_weight, E=precondition)
    kinds = dict(F=forward, X=normalise, n=normed_on, N=relay, B=backward, d=dpre_on, G=gradient)
    for i in range(N_GROUPS):
        for kind, op in kinds.items():
            if kind != "d" or i not in DIRECT:
                ops[kind + str(i)] = functools.partial(op, i)
    plans = [plan_of(section) for section in range(4)]

    def step(s):
        for name, op in ops.items():
            place = [plan.index(name) if name in plan else -1 for plan in plans]
            mine = jnp.int32(place[3])
            for section in (2, 1, 0):
                mine = jnp.where(y == section, place[section], mine)
            pl.when(s == mine)(op)

    each(0, max(len(plan) for plan in plans), step)


def on_device(inputs, weights, norm_gains, cotangent, owner_table, left_roots, right_roots):
    tokens = inputs.shape[0] * inputs.shape[1]
    half = weights.shape[2]
    width = weights.shape[1]
    bf16, f32 = jnp.bfloat16, jnp.float32
    vmem, dma = pltpu.VMEM, pltpu.SemaphoreType.DMA
    steps = N_GROUPS * N_CHUNKS
    scratch = [
        vmem((width, half), bf16), vmem((half, width), bf16),
        vmem((tokens, half), bf16), vmem((tokens, half), bf16), vmem((tokens, half), bf16),
        vmem((tokens, width), bf16), vmem((tokens, half), f32), vmem((tokens, half), f32), vmem((tokens, 128), f32),
        vmem((tokens, half), bf16), vmem((tokens, half), bf16), vmem((tokens, half), bf16), vmem((tokens, half), bf16),
        vmem((tokens, 128), f32), vmem((tokens, 128), f32), vmem((tokens, half), bf16),
        [vmem((4, 4, m, 1024), bf16) for unused, m in GROUPS], [vmem((4, 4, m, 512), bf16) for unused, m in GROUPS],
        vmem((1024, 512), f32), vmem((2, 512, 512), f32),
        vmem((16, 2, 64, 256), bf16), vmem((32, 64, 256), bf16), vmem((32, 8, 128), f32), vmem((2, 1024, 256), bf16),
        vmem((2, 2, 512, 512), bf16),
        vmem((1024, 512), bf16),
        dma((8,)), dma((2,)), dma((4,)),
        dma((steps,)), dma((steps,)), dma((steps,)), dma((steps,)),
        dma((steps,)), dma((steps,)), dma((steps,)), dma((steps,)), dma((N_GROUPS,)), dma((N_GROUPS,)),
        dma((N_GROUPS * 4,)), dma((N_GROUPS * 4,)), dma((N_GROUPS * 4,)), dma((N_GROUPS * 4,)),
        dma((N_GROUPS * 16,)), dma((N_GROUPS * 16,)), dma((N_GROUPS * 4,)), dma((N_GROUPS * 4,)),
        dma((N_GROUPS,)), dma((N_GROUPS,)),
        dma((16,)), dma((16,)), dma((16,)), dma((16,)), dma((16,)), dma((16,)), dma((4,)), dma((4,)),
    ]
    in_vmem = pl.BlockSpec(memory_space=pltpu.VMEM)
    in_hbm = pl.BlockSpec(memory_space=pl.ANY)
    result = pl.pallas_call(
        kernel,
        out_shape=[jax.ShapeDtypeStruct((256, half // 2), bf16)] * 2,
        in_specs=[pl.BlockSpec(memory_space=pltpu.SMEM), in_hbm, in_hbm, in_vmem, in_hbm, in_hbm, in_hbm],
        out_specs=[in_hbm, in_hbm],
        scratch_shapes=scratch,
        compiler_params=pltpu.CompilerParams(
            collective_id=0, has_side_effects=True, vmem_limit_bytes=62 * 2**20
        ),
    )(
        owner_table.reshape(-1), inputs.reshape(tokens, half), weights[0], norm_gains,
        cotangent.reshape(tokens, half), left_roots[0, 0], right_roots[0, 0],
    )
    return jnp.concatenate(result, axis=1)[None]


def solution(mesh):
    return jax.shard_map(
        on_device,
        mesh=mesh,
        in_specs=(
            P(None, "dp", "tensor"),
            P("pipe", None, "tensor"),
            P("pipe", None),
            P(None, "dp", "tensor"),
            P("pipe", "tensor", None),
            P("pipe", "tensor", "dp", None, None),
            P("pipe", "tensor", "dp", None, None),
        ),
        out_specs=P("pipe", "dp", "tensor"),
        check_vma=False,
    )
```

```python
import functools

import jax
import jax.numpy as jnp
from jax import lax
from jax.experimental import pallas as pl
from jax.experimental.pallas import tpu as pltpu
from jax.sharding import PartitionSpec as P

MESH = pl.DeviceIdType.MESH
norm_eps = 1e-05
GROUPS = ((0, 48), (48, 48), (96, 32))
N_GROUPS = len(GROUPS)
CHUNK = 512
N_CHUNKS = 4
DIRECT = (1, 2)
RING = (0, 1, 2)


def remote(src, dst, send, recv, target):
    return pltpu.make_async_remote_copy(
        src_ref=src, dst_ref=dst, send_sem=send, recv_sem=recv, device_id=target, device_id_type=MESH
    )


def each(low, high, body):
    def step(index, carry):
        body(index)
        return carry

    lax.fori_loop(low, high, step, 0)


def plan_of(section):
    groups = range(N_GROUPS)

    def every(kind):
        return [kind + str(i) for i in groups]

    if section == 0:
        plan = ["F0", "X0", "R1"]
        for i in groups[1:]:
            plan += ["F%d" % i, "X%d" % i, "n%d" % (i - 1)]
        plan += ["R2", "n%d" % (N_GROUPS - 1)] + every("m") + every("N")
        for i in groups:
            plan += ["B%d" % i]
            if i < N_GROUPS - 1:
                plan += ["d%d" % i] + ["G%d" % (i - 1)] * (i > 0)
            if i == N_GROUPS - 2:
                plan += ["U"]
        plan += ["d%d" % (N_GROUPS - 1)]
    elif section == 1:
        plan = ["R1"]
        for i in groups:
            plan += ["F%d" % i, "X%d" % i] + (["n%d" % (i - 1)] if i > 0 else ["R2"])
        plan += ["n%d" % (N_GROUPS - 1), "m0", "T"] + every("m")[1:]
        for i in groups:
            plan += ["B%d" % i, "d%d" % i]
        plan += every("N") + ["U"]
    elif section == 2:
        plan = ["R1", "T"]
        for i in groups:
            plan += ["F%d" % i, "X%d" % i] + ["R2"] * (i == 0)
        for i in groups:
            plan += ["B%d" % i] + ["m%d" % (i - 1)] * (i > 0) + ["n%d" % i] + ["d%d" % (i - 1)] * (i > 0)
        plan += ["d%d" % (N_GROUPS - 1), "U", "m%d" % (N_GROUPS - 1)] + every("N")
    else:
        plan = ["R1", "T", "R2"]
        for i in groups:
            if i < N_GROUPS - 1:
                plan += ["F%d" % i, "B%d" % i, "X%d" % i]
            else:
                plan += ["F%d" % i, "X%d" % i, "B%d" % i]
            if i > 0:
                plan += ["m%d" % (i - 2)] * (i > 1) + ["n%d" % (i - 1), "d%d" % (i - 1)]
        last = N_GROUPS - 1
        plan += ["U", "n%d" % last, "d%d" % last, "m%d" % (last - 1), "m%d" % last] + every("N")
    plan += [name for name in every("G") if name not in plan]
    plan += ["E"]
    without = ["d%d" % i for i in DIRECT] + ["m%d" % i for i in groups if i not in RING]
    return [name for name in plan if name not in without]


def kernel(
    order, inputs, weight_hbm, gain, cotangent, left_hbm, right_hbm, out_left, out_right,
    w, wt, h_in, h_sib, h_out, normed, pre, slope, scales, g_in, g_out, dns_out, dns_in, stat_out, stat_in, dpre,
    nrm, dpa, total, stage, frag_out, frag_mid, diag_mid, packed, roots, blocks,
    w_sem, io_sem, stage_sem, yf_s, yf_r, sh_s, sh_r, yb_s, yb_r, dn_s, dn_r, st_s, st_r,
    nr_s, nr_r, ns_s, ns_r, nh_s, nh_r, dp_s, dp_r, ds_s, ds_r, sn_s, sn_r, r1_s, r1_r, rd_s, rd_r, r2_s, r2_r, fin_s, fin_r,
):
    y = lax.axis_index("pipe")
    k = lax.axis_index("dp")
    t = lax.axis_index("tensor")
    x, z = k // 4, lax.rem(k, 4)
    half = w.shape[1]
    width = w.shape[0]
    block = 512
    frag_rows = 64
    sibling = {"tensor": 1 - t}
    up = {"pipe": lax.rem(y + 1, 4)}
    down = {"pipe": lax.rem(y + 3, 4)}

    def peer(j):
        px = lax.rem(x + j // 4, 4)
        pz = lax.rem(z + lax.rem(j, 4), 4)
        return px, pz, {"dp": px * 4 + pz}

    own0 = pl.multiple_of(t * half, half)
    oth0 = pl.multiple_of((1 - t) * half, half)

    def w_copy(c):
        start = jnp.where(c < N_CHUNKS, own0, oth0) + lax.rem(c, N_CHUNKS) * CHUNK
        rows = pl.ds(pl.multiple_of(start, CHUNK), CHUNK)
        return pltpu.make_async_copy(weight_hbm.at[rows], w.at[rows], w_sem.at[c])

    def stage_copy(i):
        source = (left_hbm, right_hbm)[i % 2]
        return pltpu.make_async_copy(source.at[i // 2], stage.at[i % 2], stage_sem.at[i])

    in_copy = pltpu.make_async_copy(inputs, h_in, io_sem.at[0])
    cot_copy = pltpu.make_async_copy(cotangent, g_in, io_sem.at[1])

    @pl.when(y == 0)
    def _():
        in_copy.start()

    @pl.when(y == 3)
    def _():
        cot_copy.start()

    def stage_start():
        for i in range(2):
            stage_copy(i).start()

    pl.when(y > 0)(stage_start)
    each(0, 2 * N_CHUNKS, lambda c: w_copy(c).start())
    pl.when(y == 0)(stage_start)

    barrier = pltpu.get_barrier_semaphore()
    for target in (sibling, up, down):
        pl.semaphore_signal(barrier, inc=1, device_id=target, device_id_type=MESH)
    each(1, 16, lambda j: pl.semaphore_signal(barrier, inc=1, device_id=peer(j)[2], device_id_type=MESH))
    pl.semaphore_wait(barrier, 18)

    def cols(c):
        return pl.ds(c * CHUNK, CHUNK)

    def forward_copy(i, c):
        off, m = GROUPS[i]
        n = i * N_CHUNKS + c
        rows = pl.ds(off, m)
        return remote(h_out.at[rows, cols(c)], h_in.at[rows, cols(c)], yf_s.at[n], yf_r.at[n], up)

    def share_copy(i, c):
        off, m = GROUPS[i]
        n = i * N_CHUNKS + c
        rows = pl.ds(off, m)
        return remote(h_in.at[rows, cols(c)], h_sib.at[rows, cols(c)], sh_s.at[n], sh_r.at[n], sibling)

    def backward_copy(i, c):
        off, m = GROUPS[i]
        n = i * N_CHUNKS + c
        rows = pl.ds(off, m)
        return remote(g_out.at[rows, cols(c)], g_in.at[rows, cols(c)], yb_s.at[n], yb_r.at[n], down)

    def dnorm_copy(i, c):
        off, m = GROUPS[i]
        n = i * N_CHUNKS + c
        rows = pl.ds(off, m)
        return remote(dns_out.at[rows, cols(c)], dns_in.at[rows, cols(c)], dn_s.at[n], dn_r.at[n], sibling)

    def stat_copy(i):
        rows = pl.ds(*GROUPS[i])
        return remote(stat_out.at[rows], stat_in.at[rows], st_s.at[i], st_r.at[i], sibling)

    own_band = pl.ds(pl.multiple_of(t * block, block), block)

    def normed_copy(i, d):
        px, pz, target = peer(4 * d)
        columns = pl.ds(pl.multiple_of((2 * px + t) * block, block), block)
        n = i * 4 + d
        return remote(
            normed.at[pl.ds(*GROUPS[i]), columns], nrm[i].at[d, 0, :, own_band], nr_s.at[n], nr_r.at[n], target
        )

    def normed_spread(i, d):
        n = i * 4 + d
        return remote(
            nrm[i].at[:, 0, :, own_band], nrm[i].at[:, d, :, own_band], ns_s.at[n], ns_r.at[n], peer(d)[2]
        )

    def spread_ways(i):
        return (1, 3) if i in RING else (1, 2, 3)

    def normed_hand_on(i, d):
        half_band = pl.ds(pl.multiple_of(t * block + (d // 2) * (block // 2), block // 2), block // 2)
        n = i * 4 + d
        return remote(
            nrm[i].at[:, d, :, half_band], nrm[i].at[:, 2, :, half_band], nh_s.at[n], nh_r.at[n], peer(d)[2]
        )

    def relay_copy(i):
        part = nrm[i].at[:, :, :, own_band]
        return remote(part, part, sn_s.at[i], sn_r.at[i], sibling)

    def dpre_copy(i, j):
        px, pz, target = peer(j)
        columns = pl.ds(pl.multiple_of(pz * block, block), block)
        n = i * 16 + j
        return remote(
            dpre.at[pl.ds(*GROUPS[i]), columns], dpa[i].at[j // 4, lax.rem(j, 4)], dp_s.at[n], dp_r.at[n], target
        )

    def dpre_spread(i, d):
        n = i * 4 + d
        return remote(dpa[i].at[0], dpa[i].at[d], ds_s.at[n], ds_r.at[n], peer(4 * d)[2])

    def dpre_peers(i):
        return 16 if i in DIRECT else 4

    def scatter_copy(j):
        px, pz, target = peer(j)
        return remote(
            frag_out.at[px * 4 + pz], frag_mid.at[pl.ds(2 * k, 2)], r1_s.at[j], r1_r.at[j], target
        )

    def diag_copy(j):
        part = diag_mid.at[pl.ds(2 * k, 2)]
        return remote(part, part, rd_s.at[j], rd_r.at[j], peer(j)[2])

    def gather_copy(j):
        px, pz, target = peer(j)
        rows = pl.ds(pl.multiple_of(k * frag_rows, frag_rows), frag_rows)
        return remote(frag_out.at[px * 4 + pz], packed.at[:, rows], r2_s.at[j], r2_r.at[j], target)

    def final_copy(d, out=out_left):
        pz = lax.rem(z + d, 4)
        rows = pl.ds(pl.multiple_of(pz * 256, 256), 256)
        columns = pl.ds(pl.multiple_of(lax.rem(z, 2) * block, block), block)
        return remote(blocks.at[rows], out.at[:, columns], fin_s.at[d], fin_r.at[d], {"dp": x * 4 + pz})

    row_of = lax.broadcasted_iota(jnp.int32, (128, 128), 0)
    col_of = lax.broadcasted_iota(jnp.int32, (128, 128), 1)

    def roots_out():
        for i in range(4):
            stage_copy(i).wait()
            values = stage[i % 2].astype(jnp.bfloat16)

            def square(a, b):
                return values[a * 128 : a * 128 + 128, b * 128 : b * 128 + 128]

            def fold(a, b):
                return jnp.where(col_of >= row_of, square(a, a).astype(jnp.float32), square(b, b).astype(jnp.float32))

            for n in range(2):
                corner = jnp.where(col_of == row_of, square(2 * n + 1, 2 * n + 1).astype(jnp.float32), 0.0)
                row = 2 * (i % 2) + n
                diag_mid[2 * k + i // 2, row : row + 1, :] = jnp.sum(corner, axis=0, keepdims=True)
            upper = [
                values[:128, 128:384],
                jnp.concatenate([square(0, 3), square(1, 2)], axis=1),
                jnp.concatenate([square(1, 3), square(2, 3)], axis=1),
                jnp.concatenate([fold(0, 1), fold(2, 3)], axis=1).astype(jnp.bfloat16),
            ]
            first = 8 * (i % 2)
            frag_out[first : first + 8, i // 2] = jnp.concatenate(upper, axis=0).reshape(8, frag_rows, 256)
            if i < 2:
                stage_copy(i + 2).start()
        each(1, 16, lambda j: scatter_copy(j).start())
        each(1, 16, lambda j: diag_copy(j).start())
        frag_mid[pl.ds(2 * k, 2)] = frag_out[k]

    def roots_on():
        each(1, 16, lambda j: scatter_copy(j).wait_send())
        each(1, 16, lambda j: scatter_copy(j).wait_recv())
        each(1, 16, lambda j: diag_copy(j).wait_send())
        each(1, 16, lambda j: diag_copy(j).wait_recv())

        def pick(j):
            px, pz, unused = peer(j)
            for i in range(2):
                slot = order[(2 * px + i) * 4 + pz]
                frag_out[px * 4 + pz, i] = frag_mid[slot]

        each(0, 16, pick)
        each(1, 16, lambda j: gather_copy(j).start())
        rows = pl.ds(pl.multiple_of(k * frag_rows, frag_rows), frag_rows)
        packed[:, rows] = frag_out[k]

    def unpack():
        each(1, 16, lambda j: gather_copy(j).wait_recv())

        def one(n):
            i, side = n // 2, lax.rem(n, 2)
            root = roots.at[i, side]
            diagonals = diag_mid[order[(2 * x + i) * 4 + z]]

            def place(a, b, square):
                root[a * 128 : a * 128 + 128, b * 128 : b * 128 + 128] = square

            def rows(r):
                return packed[i, pl.ds(pl.multiple_of(side * 512 + r * 128, 128), 128), :]

            for r, pair in enumerate((((0, 1), (0, 2)), ((0, 3), (1, 2)), ((1, 3), (2, 3)))):
                both = rows(r)
                for (a, b), square in zip(pair, (both[:, :128], both[:, 128:])):
                    place(a, b, square)
                    place(b, a, square.T)
            both = rows(3).astype(jnp.float32)
            for m, square in enumerate((both[:, :128], both[:, 128:])):
                turned = square.T
                place(2 * m, 2 * m, jnp.where(col_of >= row_of, square, turned).astype(jnp.bfloat16))
                diagonal = jnp.where(side == 0, diagonals[m : m + 1, :], diagonals[m + 2 : m + 3, :])
                second = jnp.where(col_of < row_of, square, jnp.where(col_of > row_of, turned, diagonal))
                place(2 * m + 1, 2 * m + 1, second.astype(jnp.bfloat16))

        each(0, 4, one)

    def transpose_weight():
        @pl.when(y >= 2)
        def _():
            each(0, 2 * N_CHUNKS, lambda c: w_copy(c).wait())

        def turn(c):
            part = pl.ds(pl.multiple_of(c * 256, 256), 256)
            wt[:, part] = w[part, :].T

        each(0, width // 256, turn)

    def forward(i):
        off, m = GROUPS[i]
        rows = pl.ds(off, m)
        if i == 0:
            @pl.when(y == 0)
            def _():
                in_copy.wait()
        squares = jnp.zeros((m, 1), jnp.float32)
        for c in range(N_CHUNKS):
            @pl.when(y > 0)
            def _():
                forward_copy(i, c).wait_recv()

            share_copy(i, c).start()
            if i == 0:
                @pl.when(y < 2)
                def _():
                    w_copy(c).wait()
            states = h_in[rows, cols(c)].astype(jnp.float32)
            squares += jnp.sum(states * states, axis=1, keepdims=True)
            place = pl.multiple_of(own0 + c * CHUNK, CHUNK)
            gained = (states * gain[:, pl.ds(place, CHUNK)]).astype(jnp.bfloat16)
            product = jnp.dot(gained, w[pl.ds(place, CHUNK), :], preferred_element_type=jnp.float32)
            pre[rows, :] = product if c == 0 else pre[rows, :] + product
        for c in range(N_CHUNKS):
            share_copy(i, c).wait_recv()
            if i == 0:
                @pl.when(y < 2)
                def _():
                    w_copy(N_CHUNKS + c).wait()
            states = h_sib[rows, cols(c)].astype(jnp.float32)
            squares += jnp.sum(states * states, axis=1, keepdims=True)
            place = pl.multiple_of(oth0 + c * CHUNK, CHUNK)
            gained = (states * gain[:, pl.ds(place, CHUNK)]).astype(jnp.bfloat16)
            if c < N_CHUNKS - 1:
                product = jnp.dot(gained, w[pl.ds(place, CHUNK), :], preferred_element_type=jnp.float32)
                pre[rows, :] += product
        scale = lax.rsqrt(squares / width + norm_eps)
        scales[rows, :] = jnp.broadcast_to(scale, (m, 128))
        for c in range(N_CHUNKS):
            product = jnp.dot(gained, w[pl.ds(place, CHUNK), cols(c)], preferred_element_type=jnp.float32)
            value = scale * (pre[rows, cols(c)] + product)
            logistic = 1.0 / (1.0 + jnp.exp(-value))
            h_out[rows, cols(c)] = (h_in[rows, cols(c)].astype(jnp.float32) + value * logistic).astype(jnp.bfloat16)

            @pl.when(y < 3)
            def _():
                forward_copy(i, c).start()

            pre[rows, cols(c)] = value
            slope[rows, cols(c)] = logistic * (1.0 + value * (1.0 - logistic))

    def normalise(i):
        off, m = GROUPS[i]
        rows = pl.ds(off, m)
        scale = scales[rows, 0:1]
        for c in range(N_CHUNKS):
            for source, first in ((h_in, own0), (h_sib, oth0)):
                columns = pl.ds(pl.multiple_of(first + c * CHUNK, CHUNK), CHUNK)
                states = source[rows, cols(c)].astype(jnp.float32)
                normed[rows, columns] = (states * scale * gain[:, columns]).astype(jnp.bfloat16)
        each(1, 4, lambda d: normed_copy(i, d).start())
        nrm[i][0, 0, :, own_band] = normed[rows, pl.ds(pl.multiple_of((2 * x + t) * block, block), block)]

    def normed_on(i):
        each(1, 4, lambda d: normed_copy(i, d).wait_recv())
        for d in spread_ways(i):
            normed_spread(i, d).start()

    def normed_round(i):
        for d in (1, 3):
            normed_spread(i, d).wait_recv()
            normed_hand_on(i, d).start()

    def backward(i):
        off, m = GROUPS[i]
        rows = pl.ds(off, m)
        if i == 0:
            @pl.when(y == 3)
            def _():
                cot_copy.wait()
        stat = jnp.zeros((m, 1), jnp.float32)
        for c in range(N_CHUNKS):
            @pl.when(y < 3)
            def _():
                backward_copy(i, c).wait_recv()

            grads = (g_in[rows, cols(c)].astype(jnp.float32) * slope[rows, cols(c)]).astype(jnp.bfloat16)
            dpre[rows, cols(c)] = grads
            stat += jnp.sum(grads.astype(jnp.float32) * pre[rows, cols(c)], axis=1, keepdims=True)
            if i in DIRECT:
                ahead = lax.rem(c - z + 4, 4)
                each(1, 4, lambda d: dpre_copy(i, 4 * d + ahead).start())
                pl.when(ahead > 0)(lambda: dpre_copy(i, ahead).start())

        @pl.when(y > 0)
        def _():
            stat_out[rows, :] = jnp.broadcast_to(stat, (m, 128))
            stat_copy(i).start()

        if i not in DIRECT:
            each(1, 4, lambda j: dpre_copy(i, j).start())
        dpa[i][0, 0] = dpre[rows, pl.ds(pl.multiple_of(z * block, block), block)]

        @pl.when(y > 0)
        def _():
            for c in range(N_CHUNKS):
                columns = pl.ds(pl.multiple_of(oth0 + c * CHUNK, CHUNK), CHUNK)
                part = jnp.dot(dpre[rows, :], wt[:, columns], preferred_element_type=jnp.float32)
                dns_out[rows, cols(c)] = part.astype(jnp.bfloat16)
                dnorm_copy(i, c).start()
            stat_copy(i).wait_recv()
            scale = scales[rows, 0:1]
            mean = (stat_out[rows, 0:1] + stat_in[rows, 0:1]) / width
            for c in range(N_CHUNKS):
                columns = pl.ds(pl.multiple_of(own0 + c * CHUNK, CHUNK), CHUNK)
                part = jnp.dot(dpre[rows, :], wt[:, columns], preferred_element_type=jnp.float32)
                dnorm_copy(i, c).wait_recv()
                part += dns_in[rows, cols(c)].astype(jnp.float32)
                states = h_in[rows, cols(c)].astype(jnp.float32)
                dstates = scale * (part * gain[:, columns] - states * scale * mean)
                g_out[rows, cols(c)] = (g_in[rows, cols(c)].astype(jnp.float32) + dstates).astype(jnp.bfloat16)
                backward_copy(i, c).start()

    def dpre_on(i):
        each(1, dpre_peers(i), lambda j: dpre_copy(i, j).wait_recv())
        each(1, 4, lambda d: dpre_spread(i, d).start())

    def relay(i):
        if i in RING:
            for d in (1, 3):
                normed_hand_on(i, d).wait_recv()
        else:
            each(1, 4, lambda d: normed_spread(i, d).wait_recv())
        relay_copy(i).start()

    def gradient(i):
        m = GROUPS[i][1]
        relay_copy(i).wait_recv()
        if i in DIRECT:
            each(1, 16, lambda j: dpre_copy(i, j).wait_recv())
        else:
            each(1, 4, lambda d: dpre_spread(i, d).wait_recv())
        right = dpa[i][...].reshape(16 * m, block)
        for c in range(4):
            part = pl.ds(c * 256, 256)
            left = nrm[i][:, :, :, part].reshape(16 * m, 256)
            product = lax.dot_general(left, right, (((0,), (0,)), ((), ())), preferred_element_type=jnp.float32)
            total[part, :] = product if i == 0 else total[part, :] + product

    def precondition():
        for i in range(2):
            grad = total[pl.ds(i * block, block), :].astype(jnp.bfloat16)
            lefted = jnp.dot(roots[i, 0], grad, preferred_element_type=jnp.float32).astype(jnp.bfloat16)
            result = jnp.dot(lefted, roots[i, 1], preferred_element_type=jnp.float32).astype(jnp.bfloat16)
            blocks[pl.ds(i * block, block), :] = result
            for d in range(1, 4):
                for side, out in enumerate((out_left, out_right)):
                    @pl.when((lax.rem(z + d, 4) // 2 == i) & (z // 2 == side))
                    def _():
                        final_copy(d, out).start()

        def keep_copy(out):
            rows = pl.ds(pl.multiple_of(z * 256, 256), 256)
            columns = pl.ds(pl.multiple_of(lax.rem(z, 2) * block, block), block)
            return pltpu.make_async_copy(blocks.at[rows], out.at[:, columns], io_sem.at[0])

        for side, out in enumerate((out_left, out_right)):
            pl.when(z // 2 == side)(lambda: keep_copy(out).start())

        for i in range(N_GROUPS):
            for c in range(N_CHUNKS):
                share_copy(i, c).wait_send()

                @pl.when(y < 3)
                def _():
                    forward_copy(i, c).wait_send()

                @pl.when(y > 0)
                def _():
                    backward_copy(i, c).wait_send()
                    dnorm_copy(i, c).wait_send()

            @pl.when(y > 0)
            def _():
                stat_copy(i).wait_send()

            relay_copy(i).wait_send()
            each(1, 4, lambda d: normed_copy(i, d).wait_send())
            for d in spread_ways(i):
                normed_spread(i, d).wait_send()
            if i in RING:
                for d in (1, 3):
                    normed_hand_on(i, d).wait_send()
            each(1, dpre_peers(i), lambda j: dpre_copy(i, j).wait_send())
            if i not in DIRECT:
                each(1, 4, lambda d: dpre_spread(i, d).wait_send())
        each(1, 16, lambda j: gather_copy(j).wait_send())
        for d in range(1, 4):
            final_copy(d).wait_send()
        keep_copy(out_left).wait()
        for d in range(1, 4):
            final_copy(d).wait_recv()

    ops = dict(R1=roots_out, R2=roots_on, U=unpack, T=transpose_weight, E=precondition)
    kinds = dict(F=forward, X=normalise, n=normed_on, m=normed_round, N=relay, B=backward, d=dpre_on, G=gradient)
    for i in range(N_GROUPS):
        for kind, op in kinds.items():
            if (kind != "d" or i not in DIRECT) and (kind != "m" or i in RING):
                ops[kind + str(i)] = functools.partial(op, i)
    plans = [plan_of(section) for section in range(4)]

    def step(s):
        for name, op in ops.items():
            place = [plan.index(name) if name in plan else -1 for plan in plans]
            mine = jnp.int32(place[3])
            for section in (2, 1, 0):
                mine = jnp.where(y == section, place[section], mine)
            pl.when(s == mine)(op)

    each(0, max(len(plan) for plan in plans), step)


def on_device(inputs, weights, norm_gains, cotangent, owner_table, left_roots, right_roots):
    tokens = inputs.shape[0] * inputs.shape[1]
    half = weights.shape[2]
    width = weights.shape[1]
    bf16, f32 = jnp.bfloat16, jnp.float32
    vmem, dma = pltpu.VMEM, pltpu.SemaphoreType.DMA
    steps = N_GROUPS * N_CHUNKS
    scratch = [
        vmem((width, half), bf16), vmem((half, width), bf16),
        vmem((tokens, half), bf16), vmem((tokens, half), bf16), vmem((tokens, half), bf16),
        vmem((tokens, width), bf16), vmem((tokens, half), f32), vmem((tokens, half), f32), vmem((tokens, 128), f32),
        vmem((tokens, half), bf16), vmem((tokens, half), bf16), vmem((tokens, half), bf16), vmem((tokens, half), bf16),
        vmem((tokens, 128), f32), vmem((tokens, 128), f32), vmem((tokens, half), bf16),
        [vmem((4, 4, m, 1024), bf16) for unused, m in GROUPS], [vmem((4, 4, m, 512), bf16) for unused, m in GROUPS],
        vmem((1024, 512), f32), vmem((2, 512, 512), f32),
        vmem((16, 2, 64, 256), bf16), vmem((32, 64, 256), bf16), vmem((32, 8, 128), f32), vmem((2, 1024, 256), bf16),
        vmem((2, 2, 512, 512), bf16),
        vmem((1024, 512), bf16),
        dma((8,)), dma((2,)), dma((4,)),
        dma((steps,)), dma((steps,)), dma((steps,)), dma((steps,)),
        dma((steps,)), dma((steps,)), dma((steps,)), dma((steps,)), dma((N_GROUPS,)), dma((N_GROUPS,)),
        dma((N_GROUPS * 4,)), dma((N_GROUPS * 4,)), dma((N_GROUPS * 4,)), dma((N_GROUPS * 4,)),
        dma((N_GROUPS * 4,)), dma((N_GROUPS * 4,)),
        dma((N_GROUPS * 16,)), dma((N_GROUPS * 16,)), dma((N_GROUPS * 4,)), dma((N_GROUPS * 4,)),
        dma((N_GROUPS,)), dma((N_GROUPS,)),
        dma((16,)), dma((16,)), dma((16,)), dma((16,)), dma((16,)), dma((16,)), dma((4,)), dma((4,)),
    ]
    in_vmem = pl.BlockSpec(memory_space=pltpu.VMEM)
    in_hbm = pl.BlockSpec(memory_space=pl.ANY)
    result = pl.pallas_call(
        kernel,
        out_shape=[jax.ShapeDtypeStruct((256, half // 2), bf16)] * 2,
        in_specs=[pl.BlockSpec(memory_space=pltpu.SMEM), in_hbm, in_hbm, in_vmem, in_hbm, in_hbm, in_hbm],
        out_specs=[in_hbm, in_hbm],
        scratch_shapes=scratch,
        compiler_params=pltpu.CompilerParams(
            collective_id=0, has_side_effects=True, vmem_limit_bytes=62 * 2**20
        ),
    )(
        owner_table.reshape(-1), inputs.reshape(tokens, half), weights[0], norm_gains,
        cotangent.reshape(tokens, half), left_roots[0, 0], right_roots[0, 0],
    )
    return jnp.concatenate(result, axis=1)[None]


def solution(mesh):
    return jax.shard_map(
        on_device,
        mesh=mesh,
        in_specs=(
            P(None, "dp", "tensor"),
            P("pipe", None, "tensor"),
            P("pipe", None),
            P(None, "dp", "tensor"),
            P("pipe", "tensor", None),
            P("pipe", "tensor", "dp", None, None),
            P("pipe", "tensor", "dp", None, None),
        ),
        out_specs=P("pipe", "dp", "tensor"),
        check_vma=False,
    )
```

```python
import functools

import jax
import jax.numpy as jnp
from jax import lax
from jax.experimental import pallas as pl
from jax.experimental.pallas import tpu as pltpu
from jax.sharding import PartitionSpec as P

MESH = pl.DeviceIdType.MESH
norm_eps = 1e-05
GROUPS = ((0, 48), (48, 48), (96, 32))
N_GROUPS = len(GROUPS)
CHUNK = 512
N_CHUNKS = 4
DIRECT = (1, 2)
RING = (0, 1, 2)


def remote(src, dst, send, recv, target):
    return pltpu.make_async_remote_copy(
        src_ref=src, dst_ref=dst, send_sem=send, recv_sem=recv, device_id=target, device_id_type=MESH
    )


def each(low, high, body):
    def step(index, carry):
        body(index)
        return carry

    lax.fori_loop(low, high, step, 0)


def plan_of(section):
    groups = range(N_GROUPS)

    def every(kind):
        return [kind + str(i) for i in groups]

    if section == 0:
        plan = ["F0", "X0", "R1"]
        for i in groups[1:]:
            plan += ["F%d" % i, "X%d" % i, "n%d" % (i - 1)]
        plan += ["R2", "n%d" % (N_GROUPS - 1)] + every("m") + every("N")
        for i in groups:
            plan += ["B%d" % i]
            if i < N_GROUPS - 1:
                plan += ["d%d" % i] + ["G%d" % (i - 1)] * (i > 0)
            if i == N_GROUPS - 2:
                plan += ["U"]
        plan += ["d%d" % (N_GROUPS - 1)]
    elif section == 1:
        plan = ["R1"]
        for i in groups:
            plan += ["F%d" % i, "X%d" % i] + (["n%d" % (i - 1)] if i > 0 else ["R2"])
        plan += ["n%d" % (N_GROUPS - 1), "m0", "T"] + every("m")[1:]
        for i in groups:
            plan += ["B%d" % i, "d%d" % i]
        plan += every("N") + ["U"]
    elif section == 2:
        plan = ["R1", "T"]
        for i in groups:
            plan += ["F%d" % i, "X%d" % i] + ["R2"] * (i == 0)
        for i in groups:
            plan += ["B%d" % i] + ["m%d" % (i - 1)] * (i > 0) + ["n%d" % i] + ["d%d" % (i - 1)] * (i > 0)
        plan += ["d%d" % (N_GROUPS - 1), "U", "m%d" % (N_GROUPS - 1)] + every("N")
    else:
        plan = ["R1", "T", "R2"]
        for i in groups:
            if i < N_GROUPS - 1:
                plan += ["F%d" % i, "B%d" % i, "X%d" % i]
            else:
                plan += ["F%d" % i, "X%d" % i, "B%d" % i]
            if i > 0:
                plan += ["m%d" % (i - 2)] * (i > 1) + ["n%d" % (i - 1), "d%d" % (i - 1)]
        last = N_GROUPS - 1
        plan += ["U", "n%d" % last, "d%d" % last, "m%d" % (last - 1), "m%d" % last] + every("N")
    plan += [name for name in every("G") if name not in plan]
    plan += ["E"]
    without = ["G%d" % (N_GROUPS - 1)] + ["d%d" % i for i in DIRECT] + ["m%d" % i for i in groups if i not in RING]
    return [name for name in plan if name not in without]


def kernel(
    order, inputs, weight_hbm, gain, cotangent, left_hbm, right_hbm, out_left, out_right,
    w, wt, h_in, h_sib, h_out, normed, pre, slope, scales, g_in, g_out, dns_out, dns_in, stat_out, stat_in, dpre,
    nrm, dpa, total, stage, frag_out, frag_mid, diag_mid, packed, roots, blocks,
    w_sem, io_sem, stage_sem, yf_s, yf_r, sh_s, sh_r, yb_s, yb_r, dn_s, dn_r, st_s, st_r,
    nr_s, nr_r, ns_s, ns_r, nh_s, nh_r, dp_s, dp_r, ds_s, ds_r, sn_s, sn_r, r1_s, r1_r, rd_s, rd_r, r2_s, r2_r, fin_s, fin_r,
):
    y = lax.axis_index("pipe")
    k = lax.axis_index("dp")
    t = lax.axis_index("tensor")
    x, z = k // 4, lax.rem(k, 4)
    half = w.shape[1]
    width = w.shape[0]
    block = 512
    frag_rows = 64
    sibling = {"tensor": 1 - t}
    up = {"pipe": lax.rem(y + 1, 4)}
    down = {"pipe": lax.rem(y + 3, 4)}

    def peer(j):
        px = lax.rem(x + j // 4, 4)
        pz = lax.rem(z + lax.rem(j, 4), 4)
        return px, pz, {"dp": px * 4 + pz}

    own0 = pl.multiple_of(t * half, half)
    oth0 = pl.multiple_of((1 - t) * half, half)

    def w_copy(c):
        start = jnp.where(c < N_CHUNKS, own0, oth0) + lax.rem(c, N_CHUNKS) * CHUNK
        rows = pl.ds(pl.multiple_of(start, CHUNK), CHUNK)
        return pltpu.make_async_copy(weight_hbm.at[rows], w.at[rows], w_sem.at[c])

    def stage_copy(i):
        source = (left_hbm, right_hbm)[i % 2]
        return pltpu.make_async_copy(source.at[i // 2], stage.at[i % 2], stage_sem.at[i])

    in_copy = pltpu.make_async_copy(inputs, h_in, io_sem.at[0])
    cot_copy = pltpu.make_async_copy(cotangent, g_in, io_sem.at[1])

    @pl.when(y == 0)
    def _():
        in_copy.start()

    @pl.when(y == 3)
    def _():
        cot_copy.start()

    def stage_start():
        for i in range(2):
            stage_copy(i).start()

    pl.when(y > 0)(stage_start)
    each(0, 2 * N_CHUNKS, lambda c: w_copy(c).start())
    pl.when(y == 0)(stage_start)

    barrier = pltpu.get_barrier_semaphore()
    for target in (sibling, up, down):
        pl.semaphore_signal(barrier, inc=1, device_id=target, device_id_type=MESH)
    each(1, 16, lambda j: pl.semaphore_signal(barrier, inc=1, device_id=peer(j)[2], device_id_type=MESH))
    pl.semaphore_wait(barrier, 18)

    def cols(c):
        return pl.ds(c * CHUNK, CHUNK)

    def forward_copy(i, c):
        off, m = GROUPS[i]
        n = i * N_CHUNKS + c
        rows = pl.ds(off, m)
        return remote(h_out.at[rows, cols(c)], h_in.at[rows, cols(c)], yf_s.at[n], yf_r.at[n], up)

    def share_copy(i, c):
        off, m = GROUPS[i]
        n = i * N_CHUNKS + c
        rows = pl.ds(off, m)
        return remote(h_in.at[rows, cols(c)], h_sib.at[rows, cols(c)], sh_s.at[n], sh_r.at[n], sibling)

    def backward_copy(i, c):
        off, m = GROUPS[i]
        n = i * N_CHUNKS + c
        rows = pl.ds(off, m)
        return remote(g_out.at[rows, cols(c)], g_in.at[rows, cols(c)], yb_s.at[n], yb_r.at[n], down)

    def dnorm_copy(i, c):
        off, m = GROUPS[i]
        n = i * N_CHUNKS + c
        rows = pl.ds(off, m)
        return remote(dns_out.at[rows, cols(c)], dns_in.at[rows, cols(c)], dn_s.at[n], dn_r.at[n], sibling)

    def stat_copy(i):
        rows = pl.ds(*GROUPS[i])
        return remote(stat_out.at[rows], stat_in.at[rows], st_s.at[i], st_r.at[i], sibling)

    own_band = pl.ds(pl.multiple_of(t * block, block), block)

    def normed_copy(i, d):
        px, pz, target = peer(4 * d)
        columns = pl.ds(pl.multiple_of((2 * px + t) * block, block), block)
        n = i * 4 + d
        return remote(
            normed.at[pl.ds(*GROUPS[i]), columns], nrm[i].at[d, 0, :, own_band], nr_s.at[n], nr_r.at[n], target
        )

    def normed_spread(i, d):
        n = i * 4 + d
        return remote(
            nrm[i].at[:, 0, :, own_band], nrm[i].at[:, d, :, own_band], ns_s.at[n], ns_r.at[n], peer(d)[2]
        )

    def spread_ways(i):
        return (1, 3) if i in RING else (1, 2, 3)

    def normed_hand_on(i, d):
        half_band = pl.ds(pl.multiple_of(t * block + (d // 2) * (block // 2), block // 2), block // 2)
        n = i * 4 + d
        return remote(
            nrm[i].at[:, d, :, half_band], nrm[i].at[:, 2, :, half_band], nh_s.at[n], nh_r.at[n], peer(d)[2]
        )

    def relay_copy(i):
        part = nrm[i].at[:, :, :, own_band]
        return remote(part, part, sn_s.at[i], sn_r.at[i], sibling)

    def dpre_copy(i, j):
        px, pz, target = peer(j)
        columns = pl.ds(pl.multiple_of(pz * block, block), block)
        n = i * 16 + j
        return remote(
            dpre.at[pl.ds(*GROUPS[i]), columns], dpa[i].at[j // 4, lax.rem(j, 4)], dp_s.at[n], dp_r.at[n], target
        )

    def dpre_spread(i, d):
        n = i * 4 + d
        return remote(dpa[i].at[0], dpa[i].at[d], ds_s.at[n], ds_r.at[n], peer(4 * d)[2])

    def dpre_peers(i):
        return 16 if i in DIRECT else 4

    def scatter_copy(j):
        px, pz, target = peer(j)
        return remote(
            frag_out.at[px * 4 + pz], frag_mid.at[pl.ds(2 * k, 2)], r1_s.at[j], r1_r.at[j], target
        )

    def diag_copy(j):
        part = diag_mid.at[pl.ds(2 * k, 2)]
        return remote(part, part, rd_s.at[j], rd_r.at[j], peer(j)[2])

    def gather_copy(j):
        px, pz, target = peer(j)
        rows = pl.ds(pl.multiple_of(k * frag_rows, frag_rows), frag_rows)
        return remote(frag_out.at[px * 4 + pz], packed.at[:, rows], r2_s.at[j], r2_r.at[j], target)

    def final_copy(d, out=out_left):
        pz = lax.rem(z + d, 4)
        rows = pl.ds(pl.multiple_of(pz * 256, 256), 256)
        columns = pl.ds(pl.multiple_of(lax.rem(z, 2) * block, block), block)
        return remote(blocks.at[rows], out.at[:, columns], fin_s.at[d], fin_r.at[d], {"dp": x * 4 + pz})

    row_of = lax.broadcasted_iota(jnp.int32, (128, 128), 0)
    col_of = lax.broadcasted_iota(jnp.int32, (128, 128), 1)

    def roots_out():
        for i in range(4):
            stage_copy(i).wait()
            values = stage[i % 2].astype(jnp.bfloat16)

            def square(a, b):
                return values[a * 128 : a * 128 + 128, b * 128 : b * 128 + 128]

            def fold(a, b):
                return jnp.where(col_of >= row_of, square(a, a).astype(jnp.float32), square(b, b).astype(jnp.float32))

            for n in range(2):
                corner = jnp.where(col_of == row_of, square(2 * n + 1, 2 * n + 1).astype(jnp.float32), 0.0)
                row = 2 * (i % 2) + n
                diag_mid[2 * k + i // 2, row : row + 1, :] = jnp.sum(corner, axis=0, keepdims=True)
            upper = [
                values[:128, 128:384],
                jnp.concatenate([square(0, 3), square(1, 2)], axis=1),
                jnp.concatenate([square(1, 3), square(2, 3)], axis=1),
                jnp.concatenate([fold(0, 1), fold(2, 3)], axis=1).astype(jnp.bfloat16),
            ]
            first = 8 * (i % 2)
            frag_out[first : first + 8, i // 2] = jnp.concatenate(upper, axis=0).reshape(8, frag_rows, 256)
            if i < 2:
                stage_copy(i + 2).start()
        each(1, 16, lambda j: scatter_copy(j).start())
        each(1, 16, lambda j: diag_copy(j).start())
        frag_mid[pl.ds(2 * k, 2)] = frag_out[k]

    def roots_on():
        each(1, 16, lambda j: scatter_copy(j).wait_send())
        each(1, 16, lambda j: scatter_copy(j).wait_recv())
        each(1, 16, lambda j: diag_copy(j).wait_send())
        each(1, 16, lambda j: diag_copy(j).wait_recv())

        def pick(j):
            px, pz, unused = peer(j)
            for i in range(2):
                slot = order[(2 * px + i) * 4 + pz]
                frag_out[px * 4 + pz, i] = frag_mid[slot]

        each(0, 16, pick)
        each(1, 16, lambda j: gather_copy(j).start())
        rows = pl.ds(pl.multiple_of(k * frag_rows, frag_rows), frag_rows)
        packed[:, rows] = frag_out[k]

    def unpack():
        each(1, 16, lambda j: gather_copy(j).wait_recv())

        def one(n):
            i, side = n // 2, lax.rem(n, 2)
            root = roots.at[i, side]
            diagonals = diag_mid[order[(2 * x + i) * 4 + z]]

            def place(a, b, square):
                root[a * 128 : a * 128 + 128, b * 128 : b * 128 + 128] = square

            def rows(r):
                return packed[i, pl.ds(pl.multiple_of(side * 512 + r * 128, 128), 128), :]

            for r, pair in enumerate((((0, 1), (0, 2)), ((0, 3), (1, 2)), ((1, 3), (2, 3)))):
                both = rows(r)
                for (a, b), square in zip(pair, (both[:, :128], both[:, 128:])):
                    place(a, b, square)
                    place(b, a, square.T)
            both = rows(3).astype(jnp.float32)
            for m, square in enumerate((both[:, :128], both[:, 128:])):
                turned = square.T
                place(2 * m, 2 * m, jnp.where(col_of >= row_of, square, turned).astype(jnp.bfloat16))
                diagonal = jnp.where(side == 0, diagonals[m : m + 1, :], diagonals[m + 2 : m + 3, :])
                second = jnp.where(col_of < row_of, square, jnp.where(col_of > row_of, turned, diagonal))
                place(2 * m + 1, 2 * m + 1, second.astype(jnp.bfloat16))

        each(0, 4, one)

    def transpose_weight():
        @pl.when(y >= 2)
        def _():
            each(0, 2 * N_CHUNKS, lambda c: w_copy(c).wait())

        def turn(c):
            part = pl.ds(pl.multiple_of(c * 256, 256), 256)
            wt[:, part] = w[part, :].T

        each(0, width // 256, turn)

    def forward(i):
        off, m = GROUPS[i]
        rows = pl.ds(off, m)
        if i == 0:
            @pl.when(y == 0)
            def _():
                in_copy.wait()
        squares = jnp.zeros((m, 1), jnp.float32)
        for c in range(N_CHUNKS):
            @pl.when(y > 0)
            def _():
                forward_copy(i, c).wait_recv()

            share_copy(i, c).start()
            if i == 0:
                @pl.when(y < 2)
                def _():
                    w_copy(c).wait()
            states = h_in[rows, cols(c)].astype(jnp.float32)
            squares += jnp.sum(states * states, axis=1, keepdims=True)
            place = pl.multiple_of(own0 + c * CHUNK, CHUNK)
            gained = (states * gain[:, pl.ds(place, CHUNK)]).astype(jnp.bfloat16)
            product = jnp.dot(gained, w[pl.ds(place, CHUNK), :], preferred_element_type=jnp.float32)
            pre[rows, :] = product if c == 0 else pre[rows, :] + product
        for c in range(N_CHUNKS):
            share_copy(i, c).wait_recv()
            if i == 0:
                @pl.when(y < 2)
                def _():
                    w_copy(N_CHUNKS + c).wait()
            states = h_sib[rows, cols(c)].astype(jnp.float32)
            squares += jnp.sum(states * states, axis=1, keepdims=True)
            place = pl.multiple_of(oth0 + c * CHUNK, CHUNK)
            gained = (states * gain[:, pl.ds(place, CHUNK)]).astype(jnp.bfloat16)
            if c < N_CHUNKS - 1:
                product = jnp.dot(gained, w[pl.ds(place, CHUNK), :], preferred_element_type=jnp.float32)
                pre[rows, :] += product
        scale = lax.rsqrt(squares / width + norm_eps)
        scales[rows, :] = jnp.broadcast_to(scale, (m, 128))
        for c in range(N_CHUNKS):
            product = jnp.dot(gained, w[pl.ds(place, CHUNK), cols(c)], preferred_element_type=jnp.float32)
            value = scale * (pre[rows, cols(c)] + product)
            logistic = 1.0 / (1.0 + jnp.exp(-value))
            h_out[rows, cols(c)] = (h_in[rows, cols(c)].astype(jnp.float32) + value * logistic).astype(jnp.bfloat16)

            @pl.when(y < 3)
            def _():
                forward_copy(i, c).start()

            pre[rows, cols(c)] = value
            slope[rows, cols(c)] = logistic * (1.0 + value * (1.0 - logistic))

    def normalise(i):
        off, m = GROUPS[i]
        rows = pl.ds(off, m)
        scale = scales[rows, 0:1]
        for c in range(N_CHUNKS):
            for source, first in ((h_in, own0), (h_sib, oth0)):
                columns = pl.ds(pl.multiple_of(first + c * CHUNK, CHUNK), CHUNK)
                states = source[rows, cols(c)].astype(jnp.float32)
                normed[rows, columns] = (states * scale * gain[:, columns]).astype(jnp.bfloat16)
        each(1, 4, lambda d: normed_copy(i, d).start())
        nrm[i][0, 0, :, own_band] = normed[rows, pl.ds(pl.multiple_of((2 * x + t) * block, block), block)]

    def normed_on(i):
        each(1, 4, lambda d: normed_copy(i, d).wait_recv())
        for d in spread_ways(i):
            normed_spread(i, d).start()

    def normed_round(i):
        for d in (1, 3):
            normed_spread(i, d).wait_recv()
            normed_hand_on(i, d).start()

    def backward(i):
        off, m = GROUPS[i]
        rows = pl.ds(off, m)
        if i == 0:
            @pl.when(y == 3)
            def _():
                cot_copy.wait()
        stat = jnp.zeros((m, 1), jnp.float32)
        for c in range(N_CHUNKS):
            @pl.when(y < 3)
            def _():
                backward_copy(i, c).wait_recv()

            grads = (g_in[rows, cols(c)].astype(jnp.float32) * slope[rows, cols(c)]).astype(jnp.bfloat16)
            dpre[rows, cols(c)] = grads
            stat += jnp.sum(grads.astype(jnp.float32) * pre[rows, cols(c)], axis=1, keepdims=True)
            if i in DIRECT:
                ahead = lax.rem(c - z + 4, 4)
                each(1, 4, lambda d: dpre_copy(i, 4 * d + ahead).start())
                pl.when(ahead > 0)(lambda: dpre_copy(i, ahead).start())

        @pl.when(y > 0)
        def _():
            stat_out[rows, :] = jnp.broadcast_to(stat, (m, 128))
            stat_copy(i).start()

        if i not in DIRECT:
            each(1, 4, lambda j: dpre_copy(i, j).start())
        dpa[i][0, 0] = dpre[rows, pl.ds(pl.multiple_of(z * block, block), block)]

        @pl.when(y > 0)
        def _():
            for c in range(N_CHUNKS):
                columns = pl.ds(pl.multiple_of(oth0 + c * CHUNK, CHUNK), CHUNK)
                part = jnp.dot(dpre[rows, :], wt[:, columns], preferred_element_type=jnp.float32)
                dns_out[rows, cols(c)] = part.astype(jnp.bfloat16)
                dnorm_copy(i, c).start()
            stat_copy(i).wait_recv()
            scale = scales[rows, 0:1]
            mean = (stat_out[rows, 0:1] + stat_in[rows, 0:1]) / width
            for c in range(N_CHUNKS):
                columns = pl.ds(pl.multiple_of(own0 + c * CHUNK, CHUNK), CHUNK)
                part = jnp.dot(dpre[rows, :], wt[:, columns], preferred_element_type=jnp.float32)
                dnorm_copy(i, c).wait_recv()
                part += dns_in[rows, cols(c)].astype(jnp.float32)
                states = h_in[rows, cols(c)].astype(jnp.float32)
                dstates = scale * (part * gain[:, columns] - states * scale * mean)
                g_out[rows, cols(c)] = (g_in[rows, cols(c)].astype(jnp.float32) + dstates).astype(jnp.bfloat16)
                backward_copy(i, c).start()

    def dpre_on(i):
        each(1, dpre_peers(i), lambda j: dpre_copy(i, j).wait_recv())
        each(1, 4, lambda d: dpre_spread(i, d).start())

    def relay(i):
        if i in RING:
            for d in (1, 3):
                normed_hand_on(i, d).wait_recv()
        else:
            each(1, 4, lambda d: normed_spread(i, d).wait_recv())
        relay_copy(i).start()

    def gradient(i, parts=range(4)):
        m = GROUPS[i][1]
        if 0 in parts:
            relay_copy(i).wait_recv()
            if i in DIRECT:
                each(1, 16, lambda j: dpre_copy(i, j).wait_recv())
            else:
                each(1, 4, lambda d: dpre_spread(i, d).wait_recv())
        right = dpa[i][...].reshape(16 * m, block)
        for c in parts:
            part = pl.ds(c * 256, 256)
            left = nrm[i][:, :, :, part].reshape(16 * m, 256)
            product = lax.dot_general(left, right, (((0,), (0,)), ((), ())), preferred_element_type=jnp.float32)
            total[part, :] = product if i == 0 else total[part, :] + product

    def precondition():
        for i in range(2):
            gradient(N_GROUPS - 1, (2 * i, 2 * i + 1))
            grad = total[pl.ds(i * block, block), :].astype(jnp.bfloat16)
            lefted = jnp.dot(roots[i, 0], grad, preferred_element_type=jnp.float32).astype(jnp.bfloat16)
            result = jnp.dot(lefted, roots[i, 1], preferred_element_type=jnp.float32).astype(jnp.bfloat16)
            blocks[pl.ds(i * block, block), :] = result
            for d in range(1, 4):
                for side, out in enumerate((out_left, out_right)):
                    @pl.when((lax.rem(z + d, 4) // 2 == i) & (z // 2 == side))
                    def _():
                        final_copy(d, out).start()

        def keep_copy(out):
            rows = pl.ds(pl.multiple_of(z * 256, 256), 256)
            columns = pl.ds(pl.multiple_of(lax.rem(z, 2) * block, block), block)
            return pltpu.make_async_copy(blocks.at[rows], out.at[:, columns], io_sem.at[0])

        for side, out in enumerate((out_left, out_right)):
            pl.when(z // 2 == side)(lambda: keep_copy(out).start())

        for i in range(N_GROUPS):
            for c in range(N_CHUNKS):
                share_copy(i, c).wait_send()

                @pl.when(y < 3)
                def _():
                    forward_copy(i, c).wait_send()

                @pl.when(y > 0)
                def _():
                    backward_copy(i, c).wait_send()
                    dnorm_copy(i, c).wait_send()

            @pl.when(y > 0)
            def _():
                stat_copy(i).wait_send()

            relay_copy(i).wait_send()
            each(1, 4, lambda d: normed_copy(i, d).wait_send())
            for d in spread_ways(i):
                normed_spread(i, d).wait_send()
            if i in RING:
                for d in (1, 3):
                    normed_hand_on(i, d).wait_send()
            each(1, dpre_peers(i), lambda j: dpre_copy(i, j).wait_send())
            if i not in DIRECT:
                each(1, 4, lambda d: dpre_spread(i, d).wait_send())
        each(1, 16, lambda j: gather_copy(j).wait_send())
        for d in range(1, 4):
            final_copy(d).wait_send()
        keep_copy(out_left).wait()
        for d in range(1, 4):
            final_copy(d).wait_recv()

    ops = dict(R1=roots_out, R2=roots_on, U=unpack, T=transpose_weight, E=precondition)
    kinds = dict(F=forward, X=normalise, n=normed_on, m=normed_round, N=relay, B=backward, d=dpre_on, G=gradient)
    for i in range(N_GROUPS):
        for kind, op in kinds.items():
            if (kind != "d" or i not in DIRECT) and (kind != "m" or i in RING) and kind + str(i) != "G%d" % (N_GROUPS - 1):
                ops[kind + str(i)] = functools.partial(op, i)
    plans = [plan_of(section) for section in range(4)]

    def step(s):
        for name, op in ops.items():
            place = [plan.index(name) if name in plan else -1 for plan in plans]
            mine = jnp.int32(place[3])
            for section in (2, 1, 0):
                mine = jnp.where(y == section, place[section], mine)
            pl.when(s == mine)(op)

    each(0, max(len(plan) for plan in plans), step)


def on_device(inputs, weights, norm_gains, cotangent, owner_table, left_roots, right_roots):
    tokens = inputs.shape[0] * inputs.shape[1]
    half = weights.shape[2]
    width = weights.shape[1]
    bf16, f32 = jnp.bfloat16, jnp.float32
    vmem, dma = pltpu.VMEM, pltpu.SemaphoreType.DMA
    steps = N_GROUPS * N_CHUNKS
    scratch = [
        vmem((width, half), bf16), vmem((half, width), bf16),
        vmem((tokens, half), bf16), vmem((tokens, half), bf16), vmem((tokens, half), bf16),
        vmem((tokens, width), bf16), vmem((tokens, half), f32), vmem((tokens, half), f32), vmem((tokens, 128), f32),
        vmem((tokens, half), bf16), vmem((tokens, half), bf16), vmem((tokens, half), bf16), vmem((tokens, half), bf16),
        vmem((tokens, 128), f32), vmem((tokens, 128), f32), vmem((tokens, half), bf16),
        [vmem((4, 4, m, 1024), bf16) for unused, m in GROUPS], [vmem((4, 4, m, 512), bf16) for unused, m in GROUPS],
        vmem((1024, 512), f32), vmem((2, 512, 512), f32),
        vmem((16, 2, 64, 256), bf16), vmem((32, 64, 256), bf16), vmem((32, 8, 128), f32), vmem((2, 1024, 256), bf16),
        vmem((2, 2, 512, 512), bf16),
        vmem((1024, 512), bf16),
        dma((8,)), dma((2,)), dma((4,)),
        dma((steps,)), dma((steps,)), dma((steps,)), dma((steps,)),
        dma((steps,)), dma((steps,)), dma((steps,)), dma((steps,)), dma((N_GROUPS,)), dma((N_GROUPS,)),
        dma((N_GROUPS * 4,)), dma((N_GROUPS * 4,)), dma((N_GROUPS * 4,)), dma((N_GROUPS * 4,)),
        dma((N_GROUPS * 4,)), dma((N_GROUPS * 4,)),
        dma((N_GROUPS * 16,)), dma((N_GROUPS * 16,)), dma((N_GROUPS * 4,)), dma((N_GROUPS * 4,)),
        dma((N_GROUPS,)), dma((N_GROUPS,)),
        dma((16,)), dma((16,)), dma((16,)), dma((16,)), dma((16,)), dma((16,)), dma((4,)), dma((4,)),
    ]
    in_vmem = pl.BlockSpec(memory_space=pltpu.VMEM)
    in_hbm = pl.BlockSpec(memory_space=pl.ANY)
    result = pl.pallas_call(
        kernel,
        out_shape=[jax.ShapeDtypeStruct((256, half // 2), bf16)] * 2,
        in_specs=[pl.BlockSpec(memory_space=pltpu.SMEM), in_hbm, in_hbm, in_vmem, in_hbm, in_hbm, in_hbm],
        out_specs=[in_hbm, in_hbm],
        scratch_shapes=scratch,
        compiler_params=pltpu.CompilerParams(
            collective_id=0, has_side_effects=True, vmem_limit_bytes=62 * 2**20
        ),
    )(
        owner_table.reshape(-1), inputs.reshape(tokens, half), weights[0], norm_gains,
        cotangent.reshape(tokens, half), left_roots[0, 0], right_roots[0, 0],
    )
    return jnp.concatenate(result, axis=1)[None]


def solution(mesh):
    return jax.shard_map(
        on_device,
        mesh=mesh,
        in_specs=(
            P(None, "dp", "tensor"),
            P("pipe", None, "tensor"),
            P("pipe", None),
            P(None, "dp", "tensor"),
            P("pipe", "tensor", None),
            P("pipe", "tensor", "dp", None, None),
            P("pipe", "tensor", "dp", None, None),
        ),
        out_specs=P("pipe", "dp", "tensor"),
        check_vma=False,
    )
```
